32 devices in a mesh: group: 2 (over y), ctx: 4 (over z), head: 2 (over x), rep: 2 (over core).
Axes of the slice: x: 2, y: 2, z: 4, core: 2. Of those that a mesh axis runs over, the one named last changes fastest.
Arguments:
- queries: bfloat16 [6144, 5120], P(('group', 'ctx', 'rep'), 'head'), parts along dimension 0, may hold values from -6 to 6
- key_vectors: bfloat16 [6144, 5120], P(('group', 'ctx', 'rep'), 'head'), parts along dimension 0, may hold values from -6 to 6
- value_vectors: bfloat16 [6144, 5120], P(('group', 'ctx', 'rep'), 'head'), parts along dimension 0, may hold values from -6 to 6
- gate_input: bfloat16 [6144, 5120], P(('group', 'ctx', 'rep'), 'head'), parts along dimension 0, may hold values from -6 to 6
- norm_gain: float32 [5120], P('head'), may hold values from 0.25 to 1.75
- decay_rate: float32 [40], P('head'), may hold values from 3.25520833e-05 to 0.03125
- band_reach: int32 [40], P('head'), may hold values from 1 to 24, as said below
Outputs:
- mixed_heads: bfloat16 [6144, 5120], P(('group', 'ctx', 'rep'), 'head'), parts along dimension 0
The draws below stay inside these ranges and needn't reach their ends.
There are 2 independent parts, one for each index of `group`. The reference program is written for one: setup_inputs(seed, part) draws one part's arguments, and reference() takes and returns one part's arrays. A program takes and returns all parts, laid end to end along the dimension named above; an argument that names none is the same for every part. Nothing has to cross between parts.
Inputs may be any that keep to these rules, and one draw needn't show every extreme that they name: `band_reach`: each head's reach is either at most 2 or exactly 24; in every draw some head has reach 2 and some head has 24.
All inputs are finite; a program needn't handle non-finite values.
Results may differ from the reference program's by a relative error of at most 0.0059.
Values may be sent and summed in bfloat16 or wider, within the bound.
No kernel may reach another device: no remote copies, remote signals or barrier semaphores. Data moves between devices by JAX's collectives and lax.ppermute only.
A program may use at most 128 MiB of HBM per device.

```python
import jax
import jax.numpy as jnp
from jax import lax

HEADS = 40
HD = 128
BLOCK = 128
REACH = 2
TOKENS = 3072
NBLOCKS = 24
FEAT = 5120


def head_classes(key):
    order = jax.random.permutation(jax.random.fold_in(key, 11), HEADS)
    full_count = jax.random.randint(jax.random.fold_in(key, 12), (), HEADS // 4, 3 * HEADS // 4 + 1)
    short_reach = jax.random.randint(jax.random.fold_in(key, 13), (HEADS,), 1, REACH + 1)
    picked = jnp.where(order < full_count, NBLOCKS, jnp.where(order == full_count, REACH, short_reach))
    return picked.astype(jnp.int32)


def draw_band_reach(key, part):
    classes = head_classes(key)
    return classes


def draw_decay_rate(key, part):
    classes = head_classes(key)
    key = jax.random.fold_in(key, 2)
    spread = jax.random.uniform(key, (HEADS,), jnp.float32)
    span_tokens = classes.astype(jnp.float32) * BLOCK
    short_low, short_high, full_low, full_high = (0.5, 4.0, 0.5, 2.3)
    short_rate = jnp.exp(jnp.log(short_low / span_tokens) + spread * jnp.log(short_high / short_low))
    full_rate = jnp.exp(jnp.log(full_low / TOKENS) + spread * jnp.log(full_high / full_low))
    return jnp.where(classes > REACH, full_rate, short_rate).astype(jnp.float32)


def steps_of(stream_key, extent, shards, smallest, largest):
    def one(dim, blocks):
        heights = jax.random.uniform(jax.random.fold_in(jax.random.fold_in(stream_key, 6), dim), (blocks,), jnp.float32, smallest / len(shards), largest / len(shards))
        return jnp.repeat(jnp.exp(heights), extent[dim] // blocks).reshape((-1,) + (1,) * (len(extent) - dim - 1))

    loudness = one(*shards[0])
    for cut in shards[1:]:
        loudness = loudness * one(*cut)
    return loudness


def bell_draw(key, extent, deviation, bound, pieces=(), kind=jnp.bfloat16):
    drawn = deviation * jax.random.normal(key, extent, jnp.float32)
    if pieces:
        drawn = drawn * steps_of(key, extent, pieces, -0.22, 0.18)
    return jnp.clip(drawn, -bound, bound).astype(kind)


def setup_inputs(seed: int = 0, part: int = 0) -> dict:
    arg_keys = jax.random.split(jax.random.key(seed), 8)
    part_splits = jax.random.split(jax.random.fold_in(arg_keys[7], part), 8)
    queries = bell_draw(part_splits[0], (TOKENS, FEAT), 1.0, 6.0, ((0, 8), (1, 2)))
    key_vectors = bell_draw(part_splits[1], (TOKENS, FEAT), 1.0, 6.0, ((0, 8), (1, 2)))
    value_vectors = bell_draw(part_splits[2], (TOKENS, FEAT), 1.0, 6.0, ((0, 8), (1, 2)))
    gate_input = bell_draw(part_splits[3], (TOKENS, FEAT), 1.0, 6.0, ((0, 8), (1, 2)))
    norm_gain = jnp.clip(1.0 + 0.15 * jax.random.normal(arg_keys[4], (FEAT,), jnp.float32), 0.25, 1.75)
    decay_rate = draw_decay_rate(jax.random.fold_in(arg_keys[7], 71), part)
    band_reach = draw_band_reach(jax.random.fold_in(arg_keys[7], 71), part)
    return {"queries": queries, "key_vectors": key_vectors, "value_vectors": value_vectors, "gate_input": gate_input, "norm_gain": norm_gain, "decay_rate": decay_rate, "band_reach": band_reach}


EPSILON = 1e-06

def head_retention(head_item):
    query_rows, key_rows, value_rows, rate_one, reach_one = head_item
    blocks_all = query_rows.shape[0] // BLOCK
    head_size = query_rows.shape[1]
    is_full = reach_one > REACH
    pad_zeros = jnp.zeros((REACH * BLOCK, head_size), key_rows.dtype)
    key_blocks = jnp.concatenate([pad_zeros, key_rows], 0).reshape(blocks_all + REACH, BLOCK, head_size)
    value_blocks = jnp.concatenate([pad_zeros, value_rows], 0).reshape(blocks_all + REACH, BLOCK, head_size)
    key_window = jnp.concatenate([key_blocks[shift_at:shift_at + blocks_all] for shift_at in range(REACH + 1)], 1)
    value_window = jnp.concatenate([value_blocks[shift_at:shift_at + blocks_all] for shift_at in range(REACH + 1)], 1)
    query_blocks = query_rows.reshape(blocks_all, BLOCK, head_size)
    block_index = jnp.arange(blocks_all, dtype=jnp.int32)
    offsets = jnp.arange(BLOCK, dtype=jnp.int32)
    window_offsets = jnp.arange((REACH + 1) * BLOCK, dtype=jnp.int32)
    query_pos = block_index[:, None] * BLOCK + offsets[None, :]
    key_pos = (block_index[:, None] - REACH) * BLOCK + window_offsets[None, :]
    distance = query_pos[:, :, None] - key_pos[:, None, :]
    block_gap = (REACH - window_offsets // BLOCK)[None, None, :]
    in_band = jnp.where(is_full, block_gap == 0, block_gap <= reach_one)
    allowed = in_band & (distance >= 0) & (key_pos[:, None, :] >= 0)
    scores = jnp.einsum('ctd,cud->ctu', query_blocks.astype(jnp.float32), key_window.astype(jnp.float32))
    fading = jnp.exp(-rate_one * jnp.maximum(distance, 0).astype(jnp.float32))
    weights = lax.optimization_barrier(jnp.where(allowed, scores * fading, 0.0).astype(jnp.bfloat16))
    near_part = jnp.einsum('ctu,cud->ctd', weights.astype(jnp.float32), value_window.astype(jnp.float32))
    key_fade = jnp.exp(-rate_one * (BLOCK - offsets).astype(jnp.float32))
    faded_keys = lax.optimization_barrier((key_blocks[REACH:].astype(jnp.float32) * key_fade[None, :, None]).astype(jnp.bfloat16))
    block_states = jnp.einsum('ctx,cty->cxy', faded_keys.astype(jnp.float32), value_blocks[REACH:].astype(jnp.float32), precision=lax.Precision.HIGHEST)
    step_fade = jnp.exp(-rate_one * BLOCK)

    def advance(carried, state_one):
        return (step_fade * carried + state_one, carried)
    unused, prior_state = lax.scan(advance, jnp.zeros((head_size, head_size), jnp.float32), block_states)
    prior_rounded = lax.optimization_barrier(prior_state.astype(jnp.bfloat16))
    query_fade = jnp.exp(-rate_one * offsets.astype(jnp.float32))
    faded_queries = lax.optimization_barrier((query_blocks.astype(jnp.float32) * query_fade[None, :, None]).astype(jnp.bfloat16))
    far_part = jnp.einsum('ctx,cxy->cty', faded_queries.astype(jnp.float32), prior_rounded.astype(jnp.float32), precision=lax.Precision.HIGHEST)
    retained = near_part + jnp.where(is_full, far_part, 0.0)
    return retained.reshape(blocks_all * BLOCK, head_size)

def reference(queries, key_vectors, value_vectors, gate_input, norm_gain, decay_rate, band_reach):
    tokens_all = queries.shape[0]

    def heads_first(rows_in):
        return rows_in.reshape(tokens_all, HEADS, HD).transpose(1, 0, 2)
    retained = lax.map(head_retention, (heads_first(queries), heads_first(key_vectors), heads_first(value_vectors), decay_rate, band_reach))
    retained = retained.transpose(1, 0, 2)
    row_mean = lax.optimization_barrier(jnp.mean(retained, axis=-1, keepdims=True))
    centred = retained - row_mean
    variance = lax.optimization_barrier(jnp.mean(centred * centred, axis=-1, keepdims=True))
    normed = centred * lax.rsqrt(variance + EPSILON)
    gate_rows = gate_input.reshape(tokens_all, HEADS, HD).astype(jnp.float32)
    mixed_rows = jax.nn.silu(gate_rows) * normed * norm_gain.reshape(HEADS, HD)[None]
    return mixed_rows.astype(jnp.bfloat16).reshape(tokens_all, FEAT)
```

```python
import jax
import jax.numpy as jnp
from jax import lax
from jax.experimental import pallas as pl
from jax.experimental.pallas import tpu as pltpu
from jax.sharding import PartitionSpec as P

BLOCK = 128
REACH = 2
EPSILON = 1e-06
F32 = jnp.float32
BF16 = jnp.bfloat16
VMEM_LIMIT = 32 * 1024 * 1024


def group_of(heads):
    return max(g for g in range(1, 6) if heads % g == 0)


def row_offsets():
    return lax.broadcasted_iota(jnp.int32, (BLOCK, BLOCK), 0).astype(F32)


def power(rate, tokens):
    return jnp.exp(jnp.full((1, BLOCK), -tokens, F32) * rate)


def states_kernel(place, rates, reaches, k_ref, v_ref, carry_ref, second_ref):
    blocks = k_ref.shape[0] // BLOCK
    group = carry_ref.shape[0]
    offsets = row_offsets()
    for g in range(group):
        head = (place[0] + pl.program_id(0)) * group + g
        rate = rates[head]
        is_full = (reaches[head] > REACH).astype(F32)
        base = jnp.exp((offsets - float(BLOCK)) * rate)
        columns = slice(g * BLOCK, (g + 1) * BLOCK)
        parts = []
        for t in range(blocks):
            faded = k_ref[t * BLOCK : (t + 1) * BLOCK, columns].astype(F32) * base
            if t == blocks - 2:
                second = faded.astype(BF16)
            if t < blocks - 1:
                faded = faded * (power(rate, (blocks - 1 - t) * BLOCK) * is_full)
            parts.append(faded.astype(BF16))
        values = v_ref[:, columns]
        dims = (((0,), (0,)), ((), ()))
        carry = lax.dot_general(jnp.concatenate(parts, 0), values, dims, preferred_element_type=F32)
        carry_ref[g] = carry.astype(BF16)
        rows = values[(blocks - 2) * BLOCK : (blocks - 1) * BLOCK]
        second_ref[g] = lax.dot_general(second, rows, dims, preferred_element_type=F32).astype(BF16)


def block_states(keys, values, rates, reaches, place, count):
    length, features = keys.shape
    size = features // rates.shape[0]
    group = group_of(count)
    rows = pl.BlockSpec((length, group * size), lambda i, place, rates, reaches: (0, place[0] + i))
    state = pl.BlockSpec((group, size, size), lambda i, place, rates, reaches: (i, 0, 0))
    shape = jax.ShapeDtypeStruct((count, size, size), BF16)
    return pl.pallas_call(
        states_kernel,
        grid_spec=pltpu.PrefetchScalarGridSpec(
            num_scalar_prefetch=3,
            grid=(count // group,),
            in_specs=[rows, rows],
            out_specs=[state, state],
        ),
        out_shape=[shape, shape],
        compiler_params=pltpu.CompilerParams(vmem_limit_bytes=VMEM_LIMIT),
        name="block_states",
    )(jnp.reshape(place * (count // group), (1,)), rates, reaches, keys, values)


def local_kernel(rates, reaches, q_ref, k_ref, v_ref, out_ref):
    length = q_ref.shape[0]
    blocks = length // BLOCK
    group = q_ref.shape[1] // BLOCK
    gap = row_offsets() - lax.broadcasted_iota(jnp.int32, (BLOCK, BLOCK), 1).astype(F32)
    causal = gap >= 0
    for g in range(group):
        head = pl.program_id(0) * group + g
        rate = rates[head]
        reach = reaches[head]
        columns = slice(g * BLOCK, (g + 1) * BLOCK)
        fading = jnp.exp(gap * (-rate))
        tables = [jnp.where(causal, fading, 0.0)]
        for back in range(1, blocks):
            tables.append(fading * (power(rate, back * BLOCK) * (reach >= back).astype(F32)))
        for t in range(blocks):
            rows = slice(t * BLOCK, (t + 1) * BLOCK)
            scores = lax.dot_general(
                q_ref[rows, columns],
                k_ref[: (t + 1) * BLOCK, columns],
                (((1,), (1,)), ((), ())),
                preferred_element_type=F32,
            )
            weights = jnp.concatenate(
                [scores[:, u * BLOCK : (u + 1) * BLOCK] * tables[t - u] for u in range(t + 1)], 1
            ).astype(BF16)
            out_ref[rows, columns] = jnp.dot(
                weights, v_ref[: (t + 1) * BLOCK, columns], preferred_element_type=F32
            )


def local_part(queries, keys, values, rates, reaches):
    length, features = queries.shape
    heads = rates.shape[0]
    size = features // heads
    group = group_of(heads)
    rows = pl.BlockSpec((length, group * size), lambda i, rates, reaches: (0, i))
    return pl.pallas_call(
        local_kernel,
        grid_spec=pltpu.PrefetchScalarGridSpec(
            num_scalar_prefetch=2, grid=(heads // group,), in_specs=[rows] * 3, out_specs=rows
        ),
        out_shape=jax.ShapeDtypeStruct((length, features), F32),
        compiler_params=pltpu.CompilerParams(vmem_limit_bytes=VMEM_LIMIT),
        cost_estimate=pl.CostEstimate(
            flops=12 * heads * BLOCK**3 * 2, bytes_accessed=10 * length * features, transcendentals=0
        ),
        name="local_part",
    )(rates, reaches, queries, keys, values)


def finish_kernel(place, rates, reaches, q_ref, g_ref, near_ref, gain_ref, carry_ref, second_ref, _, out_ref):
    blocks = q_ref.shape[0] // BLOCK
    group = carry_ref.shape[0]
    offsets = row_offsets()
    for g in range(group):
        head = (place[0] + pl.program_id(0)) * group + g
        rate = rates[head]
        reach = reaches[head]
        columns = slice(g * BLOCK, (g + 1) * BLOCK)
        fade = jnp.exp(offsets * (-rate))
        faded = [q_ref[t * BLOCK : (t + 1) * BLOCK, columns].astype(F32) * fade for t in range(blocks)]
        parts = [
            (faded[t] * (power(rate, t * BLOCK) * (reach > t).astype(F32))).astype(BF16)
            for t in range(blocks)
        ]
        far = jnp.dot(jnp.concatenate(parts, 0), carry_ref[g], preferred_element_type=F32)
        is_second = jnp.logical_and(reach >= 2, reach <= REACH).astype(F32)
        second = (faded[0] * (power(rate, BLOCK) * is_second)).astype(BF16)
        extra = jnp.dot(second, second_ref[g], preferred_element_type=F32)
        gain = gain_ref[:, columns]
        for t in range(blocks):
            rows = slice(t * BLOCK, (t + 1) * BLOCK)
            retained = near_ref[rows, columns] + far[rows]
            if t == 0:
                retained = retained + extra
            centred = retained - jnp.mean(retained, axis=-1, keepdims=True)
            variance = jnp.mean(centred * centred, axis=-1, keepdims=True)
            gate = g_ref[rows, columns].astype(F32)
            silu = gate / (1.0 + jnp.exp(-gate))
            out_ref[rows, columns] = (silu * (centred * lax.rsqrt(variance + EPSILON)) * gain).astype(BF16)


def finish(queries, gates, near, gain, rates, reaches, carry, second, place, into):
    length, features = queries.shape
    size = features // rates.shape[0]
    count = carry.shape[0]
    group = group_of(count)
    rows = pl.BlockSpec((length, group * size), lambda i, place, rates, reaches: (0, place[0] + i))
    state = pl.BlockSpec((group, size, size), lambda i, place, rates, reaches: (i, 0, 0))
    line = pl.BlockSpec((1, group * size), lambda i, place, rates, reaches: (0, place[0] + i))
    operands = [queries, gates, near, gain[None], carry, second]
    specs = [rows, rows, rows, line, state, state]
    aliases = {}
    if into is None:
        into = jnp.zeros((8, BLOCK), BF16)
    else:
        aliases = {9: 0}
    return pl.pallas_call(
        finish_kernel,
        grid_spec=pltpu.PrefetchScalarGridSpec(
            num_scalar_prefetch=3,
            grid=(count // group,),
            in_specs=specs + [pl.BlockSpec(memory_space=pl.ANY)],
            out_specs=rows,
        ),
        out_shape=jax.ShapeDtypeStruct((length, features), BF16),
        input_output_aliases=aliases,
        compiler_params=pltpu.CompilerParams(vmem_limit_bytes=VMEM_LIMIT),
        name="finish",
    )(jnp.reshape(place * (count // group), (1,)), rates, reaches, *operands, into)


def mixed(a, x, b, y):
    total = a[:, None, None] * x.astype(F32) + b[:, None, None] * y.astype(F32)
    return total.astype(BF16)


def chained(total, step_fade):
    count = lax.axis_size("ctx")
    one = jnp.ones_like(step_fade)
    current, arrived = total, None
    for hop in range(count - 1):
        got = lax.ppermute(current, "ctx", [(hop, hop + 1)])
        arrived = got if arrived is None else arrived + got
        if hop < count - 2:
            current = mixed(step_fade, got, one, total)
    return arrived


def in_two_steps(total, step_fade):
    one = jnp.ones_like(step_fade)
    first = lax.ppermute(total, "ctx", [(0, 1), (2, 3)])
    current = mixed(step_fade, first, one, total)
    near = lax.ppermute(current, "ctx", [(1, 2)])
    far = lax.ppermute(current, "ctx", [(1, 3)])
    return mixed(one, first, jnp.where(lax.axis_index("ctx") == 3, step_fade, one), near + far)


def per_device(queries, key_vectors, value_vectors, gate_input, norm_gain, decay_rate, band_reach):
    length = queries.shape[0]
    heads = decay_rate.shape[0]
    half = heads // 2
    rep = lax.axis_index("rep")
    other = 1 - rep
    away_carry, away_second = block_states(key_vectors, value_vectors, decay_rate, band_reach, other, half)
    own_carry, own_second = block_states(key_vectors, value_vectors, decay_rate, band_reach, rep, half)
    swap = [(0, 1), (1, 0)]
    from_pair = lax.ppermute(away_carry, "rep", swap)

    full = (band_reach > REACH).astype(F32)
    device_fade = lax.dynamic_slice_in_dim(full * jnp.exp(-decay_rate * float(length)), rep * half, half)
    chip_fade = lax.dynamic_slice_in_dim(full * jnp.exp(-decay_rate * float(2 * length)), rep * half, half)
    one = jnp.ones_like(device_fade)
    first = rep == 0
    total = mixed(jnp.where(first, device_fade, one), own_carry, jnp.where(first, one, device_fade), from_pair)

    cut = half * 3 // 5
    plans = [(slice(0, cut), chained), (slice(cut, half), in_two_steps if lax.axis_size("ctx") == 4 else chained)]
    own, away = [], []
    for part, plan in plans:
        arrived = plan(total[part], chip_fade[part])
        zero = jnp.zeros_like(one[part])
        is_first = first.astype(F32)
        fade = device_fade[part]
        own.append(mixed(jnp.where(first, one[part], fade), arrived, zero + (1.0 - is_first), from_pair[part]))
        sent = mixed(jnp.where(first, fade, one[part]), arrived, zero + is_first, own_carry[part])
        away.append(lax.ppermute(sent, "rep", swap))
    count = lax.axis_size("ctx") * 2
    steps = [(i, i + 1) for i in range(count - 1)]
    second_own = lax.ppermute(away_second, ("ctx", "rep"), steps)
    second_away = lax.ppermute(own_second, ("ctx", "rep"), steps)

    near = local_part(queries, key_vectors, value_vectors, decay_rate, band_reach)
    out = finish(queries, gate_input, near, norm_gain, decay_rate, band_reach, jnp.concatenate(own), second_own, rep, None)
    return finish(queries, gate_input, near, norm_gain, decay_rate, band_reach, jnp.concatenate(away), second_away, other, out)


def solution(mesh):
    rows = P(("group", "ctx", "rep"), "head")
    return jax.shard_map(
        per_device,
        mesh=mesh,
        in_specs=(rows, rows, rows, rows, P("head"), P("head"), P("head")),
        out_specs=rows,
        check_vma=False,
    )
```

```python
import functools

import jax
import jax.numpy as jnp
from jax import lax
from jax.experimental import pallas as pl
from jax.experimental.pallas import tpu as pltpu
from jax.sharding import PartitionSpec as P

BLOCK = 128
REACH = 2
EPSILON = 1e-06
F32 = jnp.float32
BF16 = jnp.bfloat16
MIB = 1024 * 1024
CHUNK = 5
CUT = 6
TRANS = (((0,), (0,)), ((), ()))
ROWS = (((1,), (1,)), ((), ()))
ANY = pl.BlockSpec(memory_space=pl.ANY)
HERE = pl.BlockSpec(memory_space=pltpu.VMEM)
SMEM = pltpu.SMEM


def chunk_of(heads):
    return max(g for g in range(1, CHUNK + 1) if heads % g == 0)


def row_offsets():
    return lax.broadcasted_iota(jnp.int32, (BLOCK, BLOCK), 0).astype(F32)


def power(rate, tokens):
    return jnp.exp(jnp.full((1, BLOCK), -tokens, F32) * rate)


def span(head, heads):
    return pl.ds(pl.multiple_of(head * BLOCK, BLOCK), heads * BLOCK)


def columns(g, heads=1):
    return slice(g * BLOCK, (g + heads) * BLOCK)


def centred(rows):
    return rows - jnp.mean(rows, axis=-1, keepdims=True)


def fetch(source, target, sem):
    copy = pltpu.make_async_copy(source, target, sem)
    copy.start()
    return copy


def real_head(relative, count):
    rep = lax.axis_index("rep")
    return rep * count + relative if relative < count else (1 - rep) * count + (relative - count)


def states_kernel(
    rate_in, reach_in, k_in, v_in, own_ref, away_ref, second_ref, k_ref, v_ref, coef_ref,
    rates, reaches, sems,
):
    heads = second_ref.shape[0]
    count = heads // 2
    blocks = k_in.shape[0] // BLOCK
    chunk = chunk_of(count)
    small = [fetch(rate_in, rates, sems.at[0]), fetch(reach_in, reaches, sems.at[1])]
    loads = []
    for j in range(heads // chunk):
        where = span(real_head(j * chunk, count), chunk)
        here = columns(j * chunk, chunk)
        loads.append(fetch(k_in.at[:, where], k_ref.at[:, here], sems.at[2 + 2 * j]))
        loads.append(fetch(v_in.at[:, where], v_ref.at[:, here], sems.at[3 + 2 * j]))
    for copy in small:
        copy.wait()
    first = (lax.axis_index("rep") == 0).astype(F32)
    last = (lax.axis_index("ctx") == 3).astype(F32)
    for g in range(count):
        head = real_head(g, count)
        is_full = (reaches[head] > REACH).astype(F32)
        device = power(rates[head], blocks * BLOCK) * is_full
        chip = power(rates[head], 2 * blocks * BLOCK) * is_full
        one = jnp.ones_like(device)
        rows = [first * device + (1.0 - first), first + (1.0 - first) * device, chip, last * chip + (1.0 - last)]
        for i, row in enumerate(rows + [one * first, one * (1.0 - first)]):
            coef_ref[i, g] = row
    offsets = row_offsets() - float(BLOCK)
    for g in range(heads):
        if g % chunk == 0:
            loads[2 * (g // chunk)].wait()
            loads[2 * (g // chunk) + 1].wait()
        head = real_head(g, count)
        rate = rates[head]
        is_full = (reaches[head] > REACH).astype(F32)
        base = jnp.exp(offsets * rate)
        parts = []
        for t in range(blocks):
            faded = k_ref[t * BLOCK : (t + 1) * BLOCK, columns(g)].astype(F32) * base
            if t == blocks - 2:
                second = faded.astype(BF16)
            if t < blocks - 1:
                faded = faded * (power(rate, (blocks - 1 - t) * BLOCK) * is_full)
            parts.append(faded.astype(BF16))
        values = v_ref[:, columns(g)]
        carry = lax.dot_general(jnp.concatenate(parts, 0), values, TRANS, preferred_element_type=F32)
        carry = centred(carry).astype(BF16)
        if g < count:
            own_ref[g] = carry
        else:
            away_ref[g - count] = carry
        rows = values[(blocks - 2) * BLOCK : (blocks - 1) * BLOCK]
        state = lax.dot_general(second, rows, TRANS, preferred_element_type=F32)
        second_ref[g] = centred(state).astype(BF16)


def block_states(keys, values, rates, reaches):
    length, features = keys.shape
    heads = rates.shape[0]
    half = jax.ShapeDtypeStruct((heads // 2, BLOCK, BLOCK), BF16)
    rows = jax.ShapeDtypeStruct((length, features), BF16)
    coefs = jax.ShapeDtypeStruct((6, heads // 2, 1, BLOCK), F32)
    return pl.pallas_call(
        states_kernel,
        in_specs=[ANY] * 4,
        out_specs=[HERE] * 6,
        out_shape=[half, half, jax.ShapeDtypeStruct((heads, BLOCK, BLOCK), BF16), rows, rows, coefs],
        scratch_shapes=[
            SMEM(rates.shape, F32),
            SMEM(reaches.shape, jnp.int32),
            pltpu.SemaphoreType.DMA((2 + 2 * (heads // chunk_of(heads // 2)),)),
        ],
        compiler_params=pltpu.CompilerParams(vmem_limit_bytes=10 * MIB),
        name="block_states",
    )(rates, reaches, keys, values)


def local_kernel(
    start, rate_in, reach_in, gain_in, q_in, g_in, k_ref, v_ref, near_ref, faded_ref, second_ref, silu_ref,
    rates, reaches, gain, q_ref, g_ref, weights, sems,
):
    length = k_ref.shape[0]
    blocks = length // BLOCK
    count = near_ref.shape[1] // BLOCK
    half = k_ref.shape[1] // BLOCK // 2
    head0 = real_head(start, half)
    where = span(head0, count)
    small = [fetch(rate_in, rates, sems.at[0]), fetch(reach_in, reaches, sems.at[1])]
    load = fetch(q_in.at[:, where], q_ref, sems.at[3])
    gates = [fetch(g_in.at[:, where], g_ref, sems.at[4]), fetch(gain_in, gain, sems.at[2])]
    for copy in small:
        copy.wait()
    offsets = row_offsets()
    gap = offsets - lax.broadcasted_iota(jnp.int32, (BLOCK, BLOCK), 1).astype(F32)
    causal = gap >= 0
    load.wait()
    for g in range(count):
        rate = rates[head0 + g]
        reach = reaches[head0 + g]
        fading = jnp.exp(gap * (-rate))
        tables = [jnp.where(causal, fading, 0.0)]
        for back in range(1, blocks):
            tables.append(fading * (power(rate, back * BLOCK) * (reach >= back).astype(F32)))
        fade = jnp.exp(offsets * (-rate))
        is_second = jnp.logical_and(reach >= 2, reach <= REACH).astype(F32)
        for t in range(blocks):
            rows = slice(t * BLOCK, (t + 1) * BLOCK)
            queries = q_ref[rows, columns(g)]
            scores = lax.dot_general(
                queries, k_ref[: (t + 1) * BLOCK, columns(start + g)], ROWS, preferred_element_type=F32
            )
            for u in range(t + 1):
                tile = slice(u * BLOCK, (u + 1) * BLOCK)
                weights[g, rows, tile] = (scores[:, tile] * tables[t - u]).astype(BF16)
            faded = queries.astype(F32) * fade
            faded_ref[rows, columns(g)] = (faded * (power(rate, t * BLOCK) * (reach > t).astype(F32))).astype(BF16)
            if t == 0:
                second_ref[:, columns(g)] = (faded * (power(rate, BLOCK) * is_second)).astype(BF16)
    for g in range(count):
        for t in range(blocks):
            rows = slice(t * BLOCK, (t + 1) * BLOCK)
            near = jnp.dot(
                weights[g, rows, : (t + 1) * BLOCK],
                v_ref[: (t + 1) * BLOCK, columns(start + g)],
                preferred_element_type=F32,
            )
            near_ref[rows, columns(g)] = centred(near)
    for copy in gates:
        copy.wait()
    for g in range(count):
        gate = g_ref[:, columns(g)].astype(F32)
        silu_ref[:, columns(g)] = gate / (1.0 + jnp.exp(-gate)) * gain[pl.ds(head0 + g, 1), :]


def local_part(start, count, queries, gates, keys, values, gain, rates, reaches):
    length = keys.shape[0]
    width = count * BLOCK
    rows = jax.ShapeDtypeStruct((length, width), BF16)
    wide = jax.ShapeDtypeStruct((length, width), F32)
    return pl.pallas_call(
        functools.partial(local_kernel, start),
        in_specs=[ANY] * 5 + [HERE] * 2,
        out_specs=[HERE] * 4,
        out_shape=[wide, rows, jax.ShapeDtypeStruct((BLOCK, width), BF16), wide],
        scratch_shapes=[
            SMEM(rates.shape, F32),
            SMEM(reaches.shape, jnp.int32),
            pltpu.VMEM(gain.shape, F32),
            pltpu.VMEM((length, width), BF16),
            pltpu.VMEM((length, width), BF16),
            pltpu.VMEM((count, length, length), BF16),
            pltpu.SemaphoreType.DMA((5,)),
        ],
        compiler_params=pltpu.CompilerParams(vmem_limit_bytes=14 * MIB),
        cost_estimate=pl.CostEstimate(flops=1, bytes_accessed=1, transcendentals=0),
        name=f"local_{start}",
    )(rates, reaches, gain, queries, gates, keys, values)


def finish_kernel(mine, parts, *refs):
    locals_in, refs = refs[: 4 * parts], refs[4 * parts :]
    carry_ref, second_ref = refs[:2]
    out_ref, retained, rows_ref, sems = refs[-4:]
    count = carry_ref.shape[0]
    blocks = out_ref.shape[0] // BLOCK
    head0 = real_head(0 if mine else count, count)
    second0 = count if mine else 0
    stores = []
    start = 0
    for j in range(parts):
        near_ref, faded_ref, fsecond_ref, silu_ref = locals_in[4 * j : 4 * j + 4]
        heads = near_ref.shape[1] // BLOCK
        for g in range(heads):
            cols = columns(g)
            here = columns(start + g)
            far = jnp.dot(faded_ref[:, cols], carry_ref[start + g], preferred_element_type=F32)
            extra = jnp.dot(fsecond_ref[:, cols], second_ref[second0 + start + g], preferred_element_type=F32)
            retained[:BLOCK, here] = near_ref[:BLOCK, cols] + far[:BLOCK] + extra
            retained[BLOCK:, here] = near_ref[BLOCK:, cols] + far[BLOCK:]
        for g in range(heads):
            for t in range(blocks):
                rows = slice(t * BLOCK, (t + 1) * BLOCK)
                parted = retained[rows, columns(start + g)]
                variance = jnp.mean(parted * parted, axis=-1, keepdims=True)
                mixed_rows = silu_ref[rows, columns(g)] * (parted * lax.rsqrt(variance + EPSILON))
                rows_ref[rows, columns(start + g)] = mixed_rows.astype(BF16)
        here = columns(start, heads)
        stores.append(fetch(rows_ref.at[:, here], out_ref.at[:, span(head0 + start, heads)], sems.at[j]))
        start += heads
    for copy in stores:
        copy.wait()


def finish(parts, carry, second, into=None):
    mine = into is None
    length = parts[0][0].shape[0]
    count = carry.shape[0]
    width = count * BLOCK
    operands = [x for part in parts for x in part] + [carry, second] + ([] if mine else [into])
    return pl.pallas_call(
        functools.partial(finish_kernel, mine, len(parts)),
        in_specs=[HERE] * (4 * len(parts) + 2) + ([] if mine else [ANY]),
        out_specs=ANY,
        out_shape=jax.ShapeDtypeStruct((length, 2 * width), BF16),
        scratch_shapes=[
            pltpu.VMEM((length, width), F32),
            pltpu.VMEM((length, width), BF16),
            pltpu.SemaphoreType.DMA((len(parts),)),
        ],
        input_output_aliases={} if mine else {4 * len(parts) + 2: 0},
        compiler_params=pltpu.CompilerParams(vmem_limit_bytes=10 * MIB),
        name="finish_own" if mine else "finish_away",
    )(*operands)


def mixed(a, x, b, y):
    total = a * x.astype(F32) + b * y.astype(F32)
    return total.astype(BF16)


def after(value, *others):
    return lax.optimization_barrier((value, *others))[0]


def per_device(queries, key_vectors, value_vectors, gate_input, norm_gain, decay_rate, band_reach):
    length = queries.shape[0]
    half = decay_rate.shape[0] // 2
    chips = lax.axis_size("ctx")
    swap = [(0, 1), (1, 0)]
    steps = [(i, i + 1) for i in range(2 * chips - 1)]
    stay = functools.partial(pltpu.with_memory_space_constraint, memory_space=pltpu.HBM)
    keys, values, queries, gates = [stay(x) for x in (key_vectors, value_vectors, queries, gate_input)]
    rates, reaches, gain = stay(decay_rate), stay(band_reach), stay(norm_gain.reshape(-1, BLOCK))

    own, away, seconds, keys, values, coefs = block_states(keys, values, rates, reaches)
    from_pair = lax.ppermute(away, "rep", swap)
    few = half // 2
    local = lambda start, count, *others: local_part(
        start, count, after(queries, *others), gates, keys, values, gain, rates, reaches
    )
    own_parts = [local(0, few, own)]
    from_pair, _ = lax.optimization_barrier((from_pair, own_parts[0][0]))

    to_mine, to_pair, chip_fade, late_fade, is_first, is_last = [coefs[i] for i in range(6)]
    one = jnp.ones((1, 1, 1), F32)
    total = mixed(to_mine, own, to_pair, from_pair)

    cut = half * CUT // 10
    chain, pair = slice(0, cut), slice(cut, half)
    hop = lambda x, *pairs: lax.ppermute(x, "ctx", list(pairs))
    step = lambda part, got: mixed(chip_fade[part], got, one, total[part])
    b1 = hop(total[chain], (0, 1))
    if chips == 4:
        a1 = hop(total[pair], (0, 1), (2, 3))
        neighbour = lambda x, *pairs: lax.ppermute(x, ("ctx", "rep"), list(pairs))
        second_late = neighbour(after(seconds, total), (3, 4), (5, 6))
        b2 = hop(step(chain, b1), (1, 2))
        a1, second_late = lax.optimization_barrier((a1, second_late))
        t1 = step(pair, a1)
        second = neighbour(after(seconds, t1), (0, 1), (2, 3), (4, 5), (6, 7), (1, 2))
        away_parts = [local(half, few, t1)]
        near, far = hop(t1, (1, 2)), hop(t1, (1, 3))
        b2, _ = lax.optimization_barrier((b2, away_parts[0][0]))
        t2 = step(chain, b2)
        b3 = hop(t2, (2, 3))
        own_parts.append(local(few, half - few, t2))
        away_parts.append(local(half + few, half - few, t2, second))
        b3, near, far, _, _ = lax.optimization_barrier((b3, near, far, own_parts[1][0], away_parts[1][0]))
        second = second + second_late
        arrived_b = b1 + b2 + b3
        arrived_a = mixed(one, a1, late_fade[pair], near + far)
    else:
        a1 = hop(total[pair], (0, 1))
        second = lax.ppermute(seconds, ("ctx", "rep"), steps)
        own_parts.append(local(few, half - few, total))
        away_parts = [local(half, few, total)]
        arrived_a, arrived_b, got_a, got_b = a1, b1, a1, b1
        for i in range(1, chips - 1):
            got_a, got_b = hop(step(pair, got_a), (i, i + 1)), hop(step(chain, got_b), (i, i + 1))
            arrived_a, arrived_b = arrived_a + got_a, arrived_b + got_b
        away_parts.append(local(half + few, half - few))
    arrived = jnp.concatenate([arrived_b, arrived_a])
    sent = mixed(to_mine, arrived, is_first, own)
    kept = mixed(to_pair, arrived, is_last, from_pair)
    got = lax.ppermute(sent, "rep", swap)
    out = finish(own_parts, kept, second)
    return finish(away_parts, got, second, out)


def solution(mesh):
    rows = P(("group", "ctx", "rep"), "head")
    return jax.shard_map(
        per_device,
        mesh=mesh,
        in_specs=(rows, rows, rows, rows, P("head"), P("head"), P("head")),
        out_specs=rows,
        check_vma=False,
    )
```

```python
import functools

import jax
import jax.numpy as jnp
from jax import lax
from jax.experimental import pallas as pl
from jax.experimental.pallas import tpu as pltpu
from jax.sharding import PartitionSpec as P

BLOCK = 128
REACH = 2
EPSILON = 1e-06
F32 = jnp.float32
BF16 = jnp.bfloat16
MIB = 1024 * 1024
CHUNK = 5
CUT = 5
TRANS = (((0,), (0,)), ((), ()))
ROWS = (((1,), (1,)), ((), ()))
ANY = pl.BlockSpec(memory_space=pl.ANY)
HERE = pl.BlockSpec(memory_space=pltpu.VMEM)
SMEM = pltpu.SMEM


def chunk_of(heads):
    return max(g for g in range(1, CHUNK + 1) if heads % g == 0)


def row_offsets():
    return lax.broadcasted_iota(jnp.int32, (BLOCK, BLOCK), 0).astype(F32)


def power(rate, tokens):
    return jnp.exp(jnp.full((1, BLOCK), -tokens, F32) * rate)


def span(head, heads):
    return pl.ds(pl.multiple_of(head * BLOCK, BLOCK), heads * BLOCK)


def columns(g, heads=1):
    return slice(g * BLOCK, (g + heads) * BLOCK)


def centred(rows):
    return rows - jnp.mean(rows, axis=-1, keepdims=True)


def fetch(source, target, sem):
    copy = pltpu.make_async_copy(source, target, sem)
    copy.start()
    return copy


def real_head(relative, count):
    rep = lax.axis_index("rep")
    return rep * count + relative if relative < count else (1 - rep) * count + (relative - count)


def states_kernel(
    rate_in, reach_in, k_in, v_in, own_ref, away_ref, second_ref, k_ref, v_ref, coef_ref,
    rates, reaches, sems,
):
    heads = second_ref.shape[0]
    count = heads // 2
    blocks = k_in.shape[0] // BLOCK
    chunk = chunk_of(count)
    small = [fetch(rate_in, rates, sems.at[0]), fetch(reach_in, reaches, sems.at[1])]
    loads = []
    for j in range(heads // chunk):
        where = span(real_head(j * chunk, count), chunk)
        here = columns(j * chunk, chunk)
        loads.append(fetch(k_in.at[:, where], k_ref.at[:, here], sems.at[2 + 2 * j]))
        loads.append(fetch(v_in.at[:, where], v_ref.at[:, here], sems.at[3 + 2 * j]))
    for copy in small:
        copy.wait()
    first = (lax.axis_index("rep") == 0).astype(F32)
    for g in range(count):
        head = real_head(g, count)
        is_full = (reaches[head] > REACH).astype(F32)
        device = power(rates[head], blocks * BLOCK) * is_full
        chip = power(rates[head], 2 * blocks * BLOCK) * is_full
        one = jnp.ones_like(device)
        rows = [first * device + (1.0 - first), first + (1.0 - first) * device, chip]
        for i, row in enumerate(rows + [one * first, one * (1.0 - first)]):
            coef_ref[i, g] = row
    offsets = row_offsets() - float(BLOCK)
    for g in range(heads):
        if g % chunk == 0:
            loads[2 * (g // chunk)].wait()
            loads[2 * (g // chunk) + 1].wait()
        head = real_head(g, count)
        rate = rates[head]
        is_full = (reaches[head] > REACH).astype(F32)
        base = jnp.exp(offsets * rate)
        parts = []
        for t in range(blocks):
            faded = k_ref[t * BLOCK : (t + 1) * BLOCK, columns(g)].astype(F32) * base
            if t == blocks - 2:
                second = faded.astype(BF16)
            if t < blocks - 1:
                faded = faded * (power(rate, (blocks - 1 - t) * BLOCK) * is_full)
            parts.append(faded.astype(BF16))
        values = v_ref[:, columns(g)]
        carry = lax.dot_general(jnp.concatenate(parts, 0), values, TRANS, preferred_element_type=F32)
        carry = centred(carry).astype(BF16)
        if g < count:
            own_ref[g] = carry
        else:
            away_ref[g - count] = carry
        rows = values[(blocks - 2) * BLOCK : (blocks - 1) * BLOCK]
        state = lax.dot_general(second, rows, TRANS, preferred_element_type=F32)
        second_ref[g] = centred(state).astype(BF16)


def block_states(keys, values, rates, reaches):
    length, features = keys.shape
    heads = rates.shape[0]
    half = jax.ShapeDtypeStruct((heads // 2, BLOCK, BLOCK), BF16)
    rows = jax.ShapeDtypeStruct((length, features), BF16)
    coefs = jax.ShapeDtypeStruct((5, heads // 2, 1, BLOCK), F32)
    return pl.pallas_call(
        states_kernel,
        in_specs=[ANY] * 4,
        out_specs=[HERE] * 6,
        out_shape=[half, half, jax.ShapeDtypeStruct((heads, BLOCK, BLOCK), BF16), rows, rows, coefs],
        scratch_shapes=[
            SMEM(rates.shape, F32),
            SMEM(reaches.shape, jnp.int32),
            pltpu.SemaphoreType.DMA((2 + 2 * (heads // chunk_of(heads // 2)),)),
        ],
        compiler_params=pltpu.CompilerParams(vmem_limit_bytes=10 * MIB),
        name="block_states",
    )(rates, reaches, keys, values)


def local_kernel(
    start, rate_in, reach_in, gain_in, q_in, g_in, k_ref, v_ref, near_ref, faded_ref, second_ref, silu_ref,
    rates, reaches, gain, q_ref, g_ref, weights, sems,
):
    length = k_ref.shape[0]
    blocks = length // BLOCK
    count = near_ref.shape[1] // BLOCK
    half = k_ref.shape[1] // BLOCK // 2
    head0 = real_head(start, half)
    where = span(head0, count)
    small = [fetch(rate_in, rates, sems.at[0]), fetch(reach_in, reaches, sems.at[1])]
    load = fetch(q_in.at[:, where], q_ref, sems.at[3])
    gates = [fetch(g_in.at[:, where], g_ref, sems.at[4]), fetch(gain_in, gain, sems.at[2])]
    for copy in small:
        copy.wait()
    offsets = row_offsets()
    gap = offsets - lax.broadcasted_iota(jnp.int32, (BLOCK, BLOCK), 1).astype(F32)
    causal = gap >= 0
    load.wait()
    for g in range(count):
        rate = rates[head0 + g]
        reach = reaches[head0 + g]
        fading = jnp.exp(gap * (-rate))
        tables = [jnp.where(causal, fading, 0.0)]
        for back in range(1, blocks):
            tables.append(fading * (power(rate, back * BLOCK) * (reach >= back).astype(F32)))
        fade = jnp.exp(offsets * (-rate))
        is_second = jnp.logical_and(reach >= 2, reach <= REACH).astype(F32)
        for t in range(blocks):
            rows = slice(t * BLOCK, (t + 1) * BLOCK)
            queries = q_ref[rows, columns(g)]
            scores = lax.dot_general(
                queries, k_ref[: (t + 1) * BLOCK, columns(start + g)], ROWS, preferred_element_type=F32
            )
            for u in range(t + 1):
                tile = slice(u * BLOCK, (u + 1) * BLOCK)
                weights[g, rows, tile] = (scores[:, tile] * tables[t - u]).astype(BF16)
            faded = queries.astype(F32) * fade
            faded_ref[rows, columns(g)] = (faded * (power(rate, t * BLOCK) * (reach > t).astype(F32))).astype(BF16)
            if t == 0:
                second_ref[:, columns(g)] = (faded * (power(rate, BLOCK) * is_second)).astype(BF16)
    for g in range(count):
        for t in range(blocks):
            rows = slice(t * BLOCK, (t + 1) * BLOCK)
            near = jnp.dot(
                weights[g, rows, : (t + 1) * BLOCK],
                v_ref[: (t + 1) * BLOCK, columns(start + g)],
                preferred_element_type=F32,
            )
            near_ref[rows, columns(g)] = centred(near)
    for copy in gates:
        copy.wait()
    for g in range(count):
        gate = g_ref[:, columns(g)].astype(F32)
        silu_ref[:, columns(g)] = gate / (1.0 + jnp.exp(-gate)) * gain[pl.ds(head0 + g, 1), :]


def local_part(start, count, queries, gates, keys, values, gain, rates, reaches):
    length = keys.shape[0]
    width = count * BLOCK
    rows = jax.ShapeDtypeStruct((length, width), BF16)
    wide = jax.ShapeDtypeStruct((length, width), F32)
    return pl.pallas_call(
        functools.partial(local_kernel, start),
        in_specs=[ANY] * 5 + [HERE] * 2,
        out_specs=[HERE] * 4,
        out_shape=[wide, rows, jax.ShapeDtypeStruct((BLOCK, width), BF16), wide],
        scratch_shapes=[
            SMEM(rates.shape, F32),
            SMEM(reaches.shape, jnp.int32),
            pltpu.VMEM(gain.shape, F32),
            pltpu.VMEM((length, width), BF16),
            pltpu.VMEM((length, width), BF16),
            pltpu.VMEM((count, length, length), BF16),
            pltpu.SemaphoreType.DMA((5,)),
        ],
        compiler_params=pltpu.CompilerParams(vmem_limit_bytes=14 * MIB),
        cost_estimate=pl.CostEstimate(flops=1, bytes_accessed=1, transcendentals=0),
        name=f"local_{start}",
    )(rates, reaches, gain, queries, gates, keys, values)


def finish_kernel(mine, parts, *refs):
    locals_in, refs = refs[: 4 * parts], refs[4 * parts :]
    carry_ref, second_ref = refs[:2]
    out_ref, retained, rows_ref, sems = refs[-4:]
    count = carry_ref.shape[0]
    blocks = out_ref.shape[0] // BLOCK
    head0 = real_head(0 if mine else count, count)
    second0 = count if mine else 0
    stores = []
    start = 0
    for j in range(parts):
        near_ref, faded_ref, fsecond_ref, silu_ref = locals_in[4 * j : 4 * j + 4]
        heads = near_ref.shape[1] // BLOCK
        for g in range(heads):
            cols = columns(g)
            here = columns(start + g)
            far = jnp.dot(faded_ref[:, cols], carry_ref[start + g], preferred_element_type=F32)
            extra = jnp.dot(fsecond_ref[:, cols], second_ref[second0 + start + g], preferred_element_type=F32)
            retained[:BLOCK, here] = near_ref[:BLOCK, cols] + far[:BLOCK] + extra
            retained[BLOCK:, here] = near_ref[BLOCK:, cols] + far[BLOCK:]
        for g in range(heads):
            for t in range(blocks):
                rows = slice(t * BLOCK, (t + 1) * BLOCK)
                parted = retained[rows, columns(start + g)]
                variance = jnp.mean(parted * parted, axis=-1, keepdims=True)
                mixed_rows = silu_ref[rows, columns(g)] * (parted * lax.rsqrt(variance + EPSILON))
                rows_ref[rows, columns(start + g)] = mixed_rows.astype(BF16)
        here = columns(start, heads)
        stores.append(fetch(rows_ref.at[:, here], out_ref.at[:, span(head0 + start, heads)], sems.at[j]))
        start += heads
    for copy in stores:
        copy.wait()


def finish(parts, carry, second, into=None):
    mine = into is None
    length = parts[0][0].shape[0]
    count = carry.shape[0]
    width = count * BLOCK
    operands = [x for part in parts for x in part] + [carry, second] + ([] if mine else [into])
    return pl.pallas_call(
        functools.partial(finish_kernel, mine, len(parts)),
        in_specs=[HERE] * (4 * len(parts) + 2) + ([] if mine else [ANY]),
        out_specs=ANY,
        out_shape=jax.ShapeDtypeStruct((length, 2 * width), BF16),
        scratch_shapes=[
            pltpu.VMEM((length, width), F32),
            pltpu.VMEM((length, width), BF16),
            pltpu.SemaphoreType.DMA((len(parts),)),
        ],
        input_output_aliases={} if mine else {4 * len(parts) + 2: 0},
        compiler_params=pltpu.CompilerParams(vmem_limit_bytes=10 * MIB),
        name="finish_own" if mine else "finish_away",
    )(*operands)


def mixed(a, x, b, y):
    total = a * x.astype(F32) + b * y.astype(F32)
    return total.astype(BF16)


def after(value, *others):
    return lax.optimization_barrier((value, *others))[0]


def per_device(queries, key_vectors, value_vectors, gate_input, norm_gain, decay_rate, band_reach):
    length = queries.shape[0]
    half = decay_rate.shape[0] // 2
    chips = lax.axis_size("ctx")
    swap = [(0, 1), (1, 0)]
    steps = [(i, i + 1) for i in range(2 * chips - 1)]
    stay = functools.partial(pltpu.with_memory_space_constraint, memory_space=pltpu.HBM)
    keys, values, queries, gates = [stay(x) for x in (key_vectors, value_vectors, queries, gate_input)]
    rates, reaches, gain = stay(decay_rate), stay(band_reach), stay(norm_gain.reshape(-1, BLOCK))

    own, away, seconds, keys, values, coefs = block_states(keys, values, rates, reaches)
    from_pair = lax.ppermute(away, "rep", swap)
    few = half // 2
    neighbour = lambda x, *pairs: lax.ppermute(x, ("ctx", "rep"), list(pairs))
    local = lambda start, count, *others: local_part(
        start, count, after(queries, *others), gates, keys, values, gain, rates, reaches
    )
    to_mine, to_pair, chip_fade, is_first, is_last = [coefs[i] for i in range(5)]
    one = jnp.ones((1, 1, 1), F32)
    total = mixed(to_mine, own, to_pair, from_pair)

    cut = half * CUT // 10
    chain, tail = slice(0, cut), slice(cut, half)
    hop = lambda x, i: lax.ppermute(x, "ctx", [(i, i + 1)])
    step = lambda part, got: mixed(chip_fade[part], got, one, total[part])
    b1 = hop(total[chain], 0)
    if chips == 4:
        a1 = hop(total[tail], 0)
        second = neighbour(after(seconds, total), (0, 1), (2, 3), (4, 5), (6, 7), (1, 2), (5, 6))
        t1 = step(chain, b1)
        b2 = hop(t1, 1)
        own_parts = [local(0, few, t1)]
        a1, _ = lax.optimization_barrier((a1, own_parts[0][0]))
        u1 = step(tail, a1)
        a2 = hop(u1, 1)
        second_late = neighbour(after(seconds, u1), (3, 4))
        away_parts = [local(half, few, u1)]
        b2, _ = lax.optimization_barrier((b2, away_parts[0][0]))
        t2 = step(chain, b2)
        b3 = hop(t2, 2)
        own_parts.append(local(few, half - few, t2))
        a2, _ = lax.optimization_barrier((a2, own_parts[1][0]))
        u2 = step(tail, a2)
        a3 = hop(u2, 2)
        away_parts.append(local(half + few, half - few, u2, second))
        a3, b3, second_late, _ = lax.optimization_barrier((a3, b3, second_late, away_parts[1][0]))
        second = second + second_late
        arrived_a, arrived_b = a1 + a2 + a3, b1 + b2 + b3
    else:
        a1 = hop(total[tail], 0)
        second = lax.ppermute(seconds, ("ctx", "rep"), steps)
        own_parts = [local(0, few), local(few, half - few, total)]
        away_parts = [local(half, few, total)]
        arrived_a, arrived_b, got_a, got_b = a1, b1, a1, b1
        for i in range(1, chips - 1):
            got_a, got_b = hop(step(tail, got_a), i), hop(step(chain, got_b), i)
            arrived_a, arrived_b = arrived_a + got_a, arrived_b + got_b
        away_parts.append(local(half + few, half - few))
    arrived = jnp.concatenate([arrived_b, arrived_a])
    sent = mixed(to_mine, arrived, is_first, own)
    kept = mixed(to_pair, arrived, is_last, from_pair)
    got = lax.ppermute(sent, "rep", swap)
    out = finish(own_parts, kept, second)
    return finish(away_parts, got, second, out)


def solution(mesh):
    rows = P(("group", "ctx", "rep"), "head")
    return jax.shard_map(
        per_device,
        mesh=mesh,
        in_specs=(rows, rows, rows, rows, P("head"), P("head"), P("head")),
        out_specs=rows,
        check_vma=False,
    )
```

```python
import functools

import jax
import jax.numpy as jnp
from jax import lax
from jax.experimental import pallas as pl
from jax.experimental.pallas import tpu as pltpu
from jax.sharding import PartitionSpec as P

BLOCK = 128
REACH = 2
EPSILON = 1e-06
F32 = jnp.float32
BF16 = jnp.bfloat16
MIB = 1024 * 1024
CHUNK = 5
TRANS = (((0,), (0,)), ((), ()))
ROWS = (((1,), (1,)), ((), ()))
ANY = pl.BlockSpec(memory_space=pl.ANY)
HERE = pl.BlockSpec(memory_space=pltpu.VMEM)
SMEM = pltpu.SMEM


def chunk_of(heads):
    return max(g for g in range(1, CHUNK + 1) if heads % g == 0)


def row_offsets():
    return lax.broadcasted_iota(jnp.int32, (BLOCK, BLOCK), 0).astype(F32)


def power(rate, tokens):
    return jnp.exp(jnp.full((1, BLOCK), -tokens, F32) * rate)


def span(head, heads):
    return pl.ds(pl.multiple_of(head * BLOCK, BLOCK), heads * BLOCK)


def columns(g, heads=1):
    return slice(g * BLOCK, (g + heads) * BLOCK)


def centred(rows):
    return rows - jnp.mean(rows, axis=-1, keepdims=True)


def fetch(source, target, sem):
    copy = pltpu.make_async_copy(source, target, sem)
    copy.start()
    return copy


def real_head(relative, count):
    rep = lax.axis_index("rep")
    return rep * count + relative if relative < count else (1 - rep) * count + (relative - count)


def states_kernel(
    rate_in, reach_in, k_in, v_in, own_ref, away_ref, second_ref, k_ref, v_ref, coef_ref, row_ref,
    rates, reaches, sems,
):
    heads = k_ref.shape[1] // BLOCK
    count = heads // 2
    blocks = k_in.shape[0] // BLOCK
    chunk = chunk_of(count)
    small = [fetch(rate_in, rates, sems.at[0]), fetch(reach_in, reaches, sems.at[1])]
    loads = []
    for j in range(heads // chunk):
        where = span(real_head(j * chunk, count), chunk)
        here = columns(j * chunk, chunk)
        loads.append(fetch(k_in.at[:, where], k_ref.at[:, here], sems.at[2 + 2 * j]))
        loads.append(fetch(v_in.at[:, where], v_ref.at[:, here], sems.at[3 + 2 * j]))
    for copy in small:
        copy.wait()
    first = (lax.axis_index("rep") == 0).astype(F32)
    one = jnp.ones((1, BLOCK), F32)
    for g in range(heads):
        head = real_head(g, count)
        row_ref[0, g] = one * rates[head]
        row_ref[1, g] = one * reaches[head].astype(F32)
    for g in range(count):
        head = real_head(g, count)
        is_full = (reaches[head] > REACH).astype(F32)
        device = power(rates[head], blocks * BLOCK) * is_full
        chip = power(rates[head], 2 * blocks * BLOCK) * is_full
        rows = [first * device + (1.0 - first), first + (1.0 - first) * device, chip]
        for i, row in enumerate(rows + [one * first, one * (1.0 - first)]):
            coef_ref[i, g] = row
    offsets = row_offsets() - float(BLOCK)
    for g in range(heads):
        if g % chunk == 0:
            loads[2 * (g // chunk)].wait()
            loads[2 * (g // chunk) + 1].wait()
        head = real_head(g, count)
        rate = rates[head]
        reach = reaches[head]
        is_full = (reach > REACH).astype(F32)
        base = jnp.exp(offsets * rate)
        parts = []
        for t in range(blocks):
            faded = k_ref[t * BLOCK : (t + 1) * BLOCK, columns(g)].astype(F32) * base
            if t == blocks - 2:
                second = faded.astype(BF16)
            if t < blocks - 1:
                faded = faded * (power(rate, (blocks - 1 - t) * BLOCK) * is_full)
            parts.append(faded.astype(BF16))
        values = v_ref[:, columns(g)]
        carry = lax.dot_general(jnp.concatenate(parts, 0), values, TRANS, preferred_element_type=F32)
        carry = centred(carry).astype(BF16)
        if g < count:
            own_ref[g] = carry
        else:
            away_ref[g - count] = carry
        rows = values[(blocks - 2) * BLOCK : (blocks - 1) * BLOCK]
        state = lax.dot_general(second, rows, TRANS, preferred_element_type=F32)
        second_ref[g] = centred(state).astype(BF16)


def block_states(keys, values, rates, reaches):
    length, features = keys.shape
    heads = rates.shape[0]
    half = jax.ShapeDtypeStruct((heads // 2, BLOCK, BLOCK), BF16)
    rows = jax.ShapeDtypeStruct((length, features), BF16)
    coefs = jax.ShapeDtypeStruct((5, heads // 2, 1, BLOCK), F32)
    lines = jax.ShapeDtypeStruct((2, heads, 1, BLOCK), F32)
    return pl.pallas_call(
        states_kernel,
        in_specs=[ANY] * 4,
        out_specs=[HERE] * 7,
        out_shape=[half, half, jax.ShapeDtypeStruct((heads, BLOCK, BLOCK), BF16), rows, rows, coefs, lines],
        scratch_shapes=[
            SMEM(rates.shape, F32),
            SMEM(reaches.shape, jnp.int32),
            pltpu.SemaphoreType.DMA((2 + 2 * (heads // chunk_of(heads // 2)),)),
        ],
        compiler_params=pltpu.CompilerParams(vmem_limit_bytes=10 * MIB),
        name="block_states",
    )(rates, reaches, keys, values)


def local_kernel(
    start, gain_ref, q_ref, g_ref, row_ref, k_ref, v_ref, near_ref, faded_ref, second_ref, silu_ref, weights
):
    length = k_ref.shape[0]
    blocks = length // BLOCK
    count = near_ref.shape[1] // BLOCK
    first = real_head(start, k_ref.shape[1] // BLOCK // 2)
    offsets = row_offsets()
    gap = offsets - lax.broadcasted_iota(jnp.int32, (BLOCK, BLOCK), 1).astype(F32)
    causal = gap >= 0
    for g in range(count):
        rate = row_ref[0, start + g]
        reach = row_ref[1, start + g]
        fading = jnp.exp(gap * (-rate))
        tables = [jnp.where(causal, fading, 0.0)]
        for back in range(1, blocks):
            tables.append(fading * (power(rate, back * BLOCK) * (reach >= back).astype(F32)))
        fade = jnp.exp(offsets * (-rate))
        seconds = jnp.logical_and(reach >= 2, reach <= REACH).astype(F32)
        for t in range(blocks):
            rows = slice(t * BLOCK, (t + 1) * BLOCK)
            queries = q_ref[rows, span(first + g, 1)]
            scores = lax.dot_general(
                queries, k_ref[: (t + 1) * BLOCK, columns(start + g)], ROWS, preferred_element_type=F32
            )
            for u in range(t + 1):
                tile = slice(u * BLOCK, (u + 1) * BLOCK)
                weights[g, rows, tile] = (scores[:, tile] * tables[t - u]).astype(BF16)
            faded = queries.astype(F32) * fade
            faded_ref[rows, columns(g)] = (faded * (power(rate, t * BLOCK) * (reach > t).astype(F32))).astype(BF16)
            if t == 0:
                second_ref[:, columns(g)] = (faded * (power(rate, BLOCK) * seconds)).astype(BF16)
    for g in range(count):
        for t in range(blocks):
            rows = slice(t * BLOCK, (t + 1) * BLOCK)
            near = jnp.dot(
                weights[g, rows, : (t + 1) * BLOCK],
                v_ref[: (t + 1) * BLOCK, columns(start + g)],
                preferred_element_type=F32,
            )
            near_ref[rows, columns(g)] = centred(near)
    for g in range(count):
        gate = g_ref[:, span(first + g, 1)].astype(F32)
        silu_ref[:, columns(g)] = gate / (1.0 + jnp.exp(-gate)) * gain_ref[pl.ds(first + g, 1), :]


def local_part(start, count, gain, queries, gates, lines, keys, values):
    length = keys.shape[0]
    width = count * BLOCK
    rows = jax.ShapeDtypeStruct((length, width), BF16)
    wide = jax.ShapeDtypeStruct((length, width), F32)
    shapes = [wide, rows, jax.ShapeDtypeStruct((BLOCK, width), BF16), wide]
    return pl.pallas_call(
        functools.partial(local_kernel, start),
        in_specs=[HERE] * 6,
        out_specs=[HERE] * len(shapes),
        out_shape=shapes,
        scratch_shapes=[
            pltpu.VMEM((count, length, length), BF16),
        ],
        compiler_params=pltpu.CompilerParams(vmem_limit_bytes=14 * MIB),
        cost_estimate=pl.CostEstimate(flops=1, bytes_accessed=1, transcendentals=0),
        name=f"local_{start}",
    )(gain, queries, gates, lines, keys, values)


def finish_kernel(starts, *refs):
    second_ref = refs[10]
    out_ref, retained, rows_ref, sems = refs[-4:]
    blocks = out_ref.shape[0] // BLOCK
    half = out_ref.shape[1] // BLOCK // 2
    done = 0
    for j, start in enumerate(starts):
        near_ref, faded_ref, factor_ref, _, carry_ref = refs[5 * j : 5 * j + 5]
        for g in range(carry_ref.shape[0]):
            cols = columns(g)
            here = columns(done + g)
            far = jnp.dot(faded_ref[:, cols], carry_ref[g], preferred_element_type=F32)
            extra = jnp.dot(factor_ref[:, cols], second_ref[(start + half) % (2 * half) + g], preferred_element_type=F32)
            retained[:BLOCK, here] = near_ref[:BLOCK, cols] + far[:BLOCK] + extra
            retained[BLOCK:, here] = near_ref[BLOCK:, cols] + far[BLOCK:]
        done += carry_ref.shape[0]
    done = 0
    stores = []
    for j, start in enumerate(starts):
        silu_ref, count = refs[5 * j + 3], refs[5 * j + 4].shape[0]
        for g in range(count):
            here = columns(done + g)
            for t in range(blocks):
                rows = slice(t * BLOCK, (t + 1) * BLOCK)
                parted = retained[rows, here]
                variance = jnp.mean(parted * parted, axis=-1, keepdims=True)
                mixed_rows = silu_ref[rows, columns(g)] * (parted * lax.rsqrt(variance + EPSILON))
                rows_ref[rows, here] = mixed_rows.astype(BF16)
        target = out_ref.at[:, span(real_head(start, half), count)]
        stores.append(fetch(rows_ref.at[:, columns(done, count)], target, sems.at[j]))
        done += count
    for copy in stores:
        copy.wait()


def finish(starts, parts, carries, second, into=None):
    length = parts[0][0].shape[0]
    width = 2 * carries[0].shape[0] * BLOCK
    features = second.shape[0] * BLOCK
    operands = [x for part, carry in zip(parts, carries) for x in (*part, carry)] + [second]
    operands += [] if into is None else [into]
    return pl.pallas_call(
        functools.partial(finish_kernel, starts),
        in_specs=[HERE] * 11 + ([] if into is None else [ANY]),
        out_specs=ANY,
        out_shape=jax.ShapeDtypeStruct((length, features), BF16),
        scratch_shapes=[
            pltpu.VMEM((length, width), F32),
            pltpu.VMEM((length, width), BF16),
            pltpu.SemaphoreType.DMA((2,)),
        ],
        input_output_aliases={} if into is None else {11: 0},
        compiler_params=pltpu.CompilerParams(vmem_limit_bytes=10 * MIB),
        name=f"finish_{starts[0]}",
    )(*operands)


def mixed(a, x, b, y):
    total = a * x.astype(F32) + b * y.astype(F32)
    return total.astype(BF16)


def after(value, *others):
    return lax.optimization_barrier((value, *others))[0]


def per_device(queries, key_vectors, value_vectors, gate_input, norm_gain, decay_rate, band_reach):
    heads = decay_rate.shape[0]
    half = heads // 2
    few = half // 2
    chips = lax.axis_size("ctx")
    stay = functools.partial(pltpu.with_memory_space_constraint, memory_space=pltpu.HBM)
    keys, values = stay(key_vectors), stay(value_vectors)
    rates, reaches, gain = stay(decay_rate), stay(band_reach), norm_gain.reshape(-1, BLOCK)
    gates = gate_input

    own, away, seconds, keys, values, coefs, lines = block_states(keys, values, rates, reaches)
    to_mine, to_pair, chip_fade, is_first, is_last = [coefs[i] for i in range(5)]
    one = jnp.ones((1, 1, 1), F32)
    early, late = slice(0, few), slice(few, half)
    swap = lambda x: lax.ppermute(x, "rep", [(0, 1), (1, 0)])
    steps = [(i, i + 1) for i in range(2 * chips - 1)]
    onward = lambda x, pairs: lax.ppermute(x, ("ctx", "rep"), pairs)
    hop = lambda x, i: lax.ppermute(x, "ctx", [(i, i + 1)])
    step = lambda part, got: mixed(chip_fade[part], got, one, total[part])

    def shared(part, got):
        sent = mixed(to_mine[part], got, is_first[part], own[part])
        kept = mixed(to_pair[part], got, is_last[part], from_pair[part])
        return kept, swap(sent)

    from_pair = swap(away)
    across = [(3, 4)] if chips == 4 else steps
    second_first = onward(seconds, across)
    total = mixed(to_mine, own, to_pair, from_pair)
    b1 = hop(total[early], 0)
    a1 = hop(total[late], 0)
    if chips == 4:
        second_rest = onward(after(seconds, total), [pair for pair in steps if pair not in across])
        part0 = local_part(0, few, gain, after(queries, total), gates, lines, keys, values)
        b1, _ = lax.optimization_barrier((b1, part0[0]))
        t1 = step(early, b1)
        b2 = hop(t1, 1)
        local = lambda start, count, *others: local_part(
            start, count, gain, after(queries, *others), gates, lines, keys, values
        )
        part2 = local(half, few, t1)
        a1, _ = lax.optimization_barrier((a1, part2[0]))
        u1 = step(late, a1)
        a2 = hop(u1, 1)
        part1 = local(few, half - few, u1)
        b2, second_first, _ = lax.optimization_barrier((b2, second_first, part1[0]))
        t2 = step(early, b2)
        b3 = hop(t2, 2)
        part3 = local(half + few, half - few, t2)
        a2, _ = lax.optimization_barrier((a2, part3[0]))
        u2 = step(late, a2)
        a3 = hop(u2, 2)
        b3, second_rest, _ = lax.optimization_barrier((b3, second_rest, u2))
        second = second_first + second_rest
        got_b = b1 + b2 + b3
        kept_b, sent_b = shared(early, got_b)
        out = finish((0, half), (part0, part2), (kept_b, sent_b), second)
        a3, out = lax.optimization_barrier((a3, out))
        got_a = a1 + a2 + a3
    else:
        part0 = local_part(0, few, gain, queries, gates, lines, keys, values)
        local = lambda start, count: local_part(start, count, gain, queries, gates, lines, keys, values)
        got_a, got_b = arrived_a, arrived_b = a1, b1
        for i in range(1, chips - 1):
            arrived_a, arrived_b = hop(step(late, arrived_a), i), hop(step(early, arrived_b), i)
            got_a, got_b = got_a + arrived_a, got_b + arrived_b
        part1, part2, part3 = local(few, half - few), local(half, few), local(half + few, half - few)
        second = second_first
        kept_b, sent_b = shared(early, got_b)
        out = finish((0, half), (part0, part2), (kept_b, sent_b), second)
    kept_a, sent_a = shared(late, got_a)
    return finish((few, half + few), (part1, part3), (kept_a, sent_a), second, out)


def solution(mesh):
    rows = P(("group", "ctx", "rep"), "head")
    return jax.shard_map(
        per_device,
        mesh=mesh,
        in_specs=(rows, rows, rows, rows, P("head"), P("head"), P("head")),
        out_specs=rows,
        check_vma=False,
    )
```

```python
import functools

import jax
import jax.numpy as jnp
from jax import lax
from jax.experimental import pallas as pl
from jax.experimental.pallas import tpu as pltpu
from jax.sharding import PartitionSpec as P

BLOCK = 128
REACH = 2
EPSILON = 1e-06
F32 = jnp.float32
BF16 = jnp.bfloat16
MIB = 1024 * 1024
CHUNK = 5
TRANS = (((0,), (0,)), ((), ()))
ROWS = (((1,), (1,)), ((), ()))
ANY = pl.BlockSpec(memory_space=pl.ANY)
HERE = pl.BlockSpec(memory_space=pltpu.VMEM)
SMEM = pltpu.SMEM


def chunk_of(heads):
    return max(g for g in range(1, CHUNK + 1) if heads % g == 0)


def row_offsets():
    return lax.broadcasted_iota(jnp.int32, (BLOCK, BLOCK), 0).astype(F32)


def power(rate, tokens):
    return jnp.exp(jnp.full((1, BLOCK), -tokens, F32) * rate)


def span(head, heads):
    return pl.ds(pl.multiple_of(head * BLOCK, BLOCK), heads * BLOCK)


def columns(g, heads=1):
    return slice(g * BLOCK, (g + heads) * BLOCK)


def centred(rows):
    return rows - jnp.mean(rows, axis=-1, keepdims=True)


def fetch(source, target, sem):
    copy = pltpu.make_async_copy(source, target, sem)
    copy.start()
    return copy


def real_head(relative, count):
    rep = lax.axis_index("rep")
    return rep * count + relative if relative < count else (1 - rep) * count + (relative - count)


def states_kernel(
    rate_in, reach_in, k_in, v_in, own_ref, away_ref, second_ref, k_ref, v_ref, coef_ref, row_ref,
    rates, reaches, sems,
):
    heads = k_ref.shape[1] // BLOCK
    count = heads // 2
    blocks = k_in.shape[0] // BLOCK
    chunk = chunk_of(count)
    small = [fetch(rate_in, rates, sems.at[0]), fetch(reach_in, reaches, sems.at[1])]
    loads = []
    for j in range(heads // chunk):
        where = span(real_head(j * chunk, count), chunk)
        here = columns(j * chunk, chunk)
        loads.append(fetch(k_in.at[:, where], k_ref.at[:, here], sems.at[2 + 2 * j]))
        loads.append(fetch(v_in.at[:, where], v_ref.at[:, here], sems.at[3 + 2 * j]))
    for copy in small:
        copy.wait()
    first = (lax.axis_index("rep") == 0).astype(F32)
    one = jnp.ones((1, BLOCK), F32)
    for g in range(heads):
        head = real_head(g, count)
        row_ref[0, g] = one * rates[head]
        row_ref[1, g] = one * reaches[head].astype(F32)
    for g in range(count):
        head = real_head(g, count)
        is_full = (reaches[head] > REACH).astype(F32)
        device = power(rates[head], blocks * BLOCK) * is_full
        chip = power(rates[head], 2 * blocks * BLOCK) * is_full
        rows = [first * device + (1.0 - first), first + (1.0 - first) * device, chip]
        for i, row in enumerate(rows + [one * first, one * (1.0 - first)]):
            coef_ref[i, g] = row
    offsets = row_offsets() - float(BLOCK)
    for g in range(heads):
        if g % chunk == 0:
            loads[2 * (g // chunk)].wait()
            loads[2 * (g // chunk) + 1].wait()
        head = real_head(g, count)
        rate = rates[head]
        reach = reaches[head]
        is_full = (reach > REACH).astype(F32)
        base = jnp.exp(offsets * rate)
        parts = []
        for t in range(blocks):
            faded = k_ref[t * BLOCK : (t + 1) * BLOCK, columns(g)].astype(F32) * base
            if t == blocks - 2:
                second = faded.astype(BF16)
            if t < blocks - 1:
                faded = faded * (power(rate, (blocks - 1 - t) * BLOCK) * is_full)
            parts.append(faded.astype(BF16))
        values = v_ref[:, columns(g)]
        carry = lax.dot_general(jnp.concatenate(parts, 0), values, TRANS, preferred_element_type=F32)
        carry = centred(carry).astype(BF16)
        if g < count:
            own_ref[g] = carry
        else:
            away_ref[g - count] = carry
        rows = values[(blocks - 2) * BLOCK : (blocks - 1) * BLOCK]
        state = lax.dot_general(second, rows, TRANS, preferred_element_type=F32)
        second_ref[g] = centred(state).astype(BF16)


def block_states(keys, values, rates, reaches):
    length, features = keys.shape
    heads = rates.shape[0]
    half = jax.ShapeDtypeStruct((heads // 2, BLOCK, BLOCK), BF16)
    rows = jax.ShapeDtypeStruct((length, features), BF16)
    coefs = jax.ShapeDtypeStruct((5, heads // 2, 1, BLOCK), F32)
    lines = jax.ShapeDtypeStruct((2, heads, 1, BLOCK), F32)
    return pl.pallas_call(
        states_kernel,
        in_specs=[ANY] * 4,
        out_specs=[HERE] * 7,
        out_shape=[half, half, jax.ShapeDtypeStruct((heads, BLOCK, BLOCK), BF16), rows, rows, coefs, lines],
        scratch_shapes=[
            SMEM(rates.shape, F32),
            SMEM(reaches.shape, jnp.int32),
            pltpu.SemaphoreType.DMA((2 + 2 * (heads // chunk_of(heads // 2)),)),
        ],
        compiler_params=pltpu.CompilerParams(vmem_limit_bytes=10 * MIB),
        name="block_states",
    )(rates, reaches, keys, values)


def local_kernel(
    start, gain_ref, q_ref, g_ref, row_ref, k_ref, v_ref, near_ref, faded_ref, second_ref, silu_ref, weights
):
    length = k_ref.shape[0]
    blocks = length // BLOCK
    count = near_ref.shape[1] // BLOCK
    first = real_head(start, k_ref.shape[1] // BLOCK // 2)
    offsets = row_offsets()
    gap = offsets - lax.broadcasted_iota(jnp.int32, (BLOCK, BLOCK), 1).astype(F32)
    causal = gap >= 0
    for g in range(count):
        rate = row_ref[0, start + g]
        reach = row_ref[1, start + g]
        fading = jnp.exp(gap * (-rate))
        tables = [jnp.where(causal, fading, 0.0)]
        for back in range(1, blocks):
            tables.append(fading * (power(rate, back * BLOCK) * (reach >= back).astype(F32)))
        fade = jnp.exp(offsets * (-rate))
        seconds = jnp.logical_and(reach >= 2, reach <= REACH).astype(F32)
        for t in range(blocks):
            rows = slice(t * BLOCK, (t + 1) * BLOCK)
            queries = q_ref[rows, span(first + g, 1)]
            scores = lax.dot_general(
                queries, k_ref[: (t + 1) * BLOCK, columns(start + g)], ROWS, preferred_element_type=F32
            )
            for u in range(t + 1):
                tile = slice(u * BLOCK, (u + 1) * BLOCK)
                weights[g, rows, tile] = (scores[:, tile] * tables[t - u]).astype(BF16)
            faded = queries.astype(F32) * fade
            faded_ref[rows, columns(g)] = (faded * (power(rate, t * BLOCK) * (reach > t).astype(F32))).astype(BF16)
            if t == 0:
                second_ref[:, columns(g)] = (faded * (power(rate, BLOCK) * seconds)).astype(BF16)
    for g in range(count):
        for t in range(blocks):
            rows = slice(t * BLOCK, (t + 1) * BLOCK)
            near = jnp.dot(
                weights[g, rows, : (t + 1) * BLOCK],
                v_ref[: (t + 1) * BLOCK, columns(start + g)],
                preferred_element_type=F32,
            )
            near_ref[rows, columns(g)] = centred(near)
    for g in range(count):
        gate = g_ref[:, span(first + g, 1)].astype(F32)
        silu_ref[:, columns(g)] = gate / (1.0 + jnp.exp(-gate)) * gain_ref[pl.ds(first + g, 1), :]


def local_part(start, count, gain, queries, gates, lines, keys, values):
    length = keys.shape[0]
    width = count * BLOCK
    rows = jax.ShapeDtypeStruct((length, width), BF16)
    wide = jax.ShapeDtypeStruct((length, width), F32)
    shapes = [wide, rows, jax.ShapeDtypeStruct((BLOCK, width), BF16), wide]
    return pl.pallas_call(
        functools.partial(local_kernel, start),
        in_specs=[HERE] * 6,
        out_specs=[HERE] * len(shapes),
        out_shape=shapes,
        scratch_shapes=[
            pltpu.VMEM((count, length, length), BF16),
        ],
        compiler_params=pltpu.CompilerParams(vmem_limit_bytes=14 * MIB),
        cost_estimate=pl.CostEstimate(flops=1, bytes_accessed=1, transcendentals=0),
        name=f"local_{start}",
    )(gain, queries, gates, lines, keys, values)


def finish_kernel(starts, *refs):
    second_ref = refs[5 * len(starts)]
    out_ref, retained, rows_ref, sems = refs[-4:]
    blocks = out_ref.shape[0] // BLOCK
    half = out_ref.shape[1] // BLOCK // 2
    done = 0
    for j, start in enumerate(starts):
        near_ref, faded_ref, factor_ref, _, carry_ref = refs[5 * j : 5 * j + 5]
        for g in range(carry_ref.shape[0]):
            cols = columns(g)
            here = columns(done + g)
            far = jnp.dot(faded_ref[:, cols], carry_ref[g], preferred_element_type=F32)
            extra = jnp.dot(factor_ref[:, cols], second_ref[(start + half) % (2 * half) + g], preferred_element_type=F32)
            retained[:BLOCK, here] = near_ref[:BLOCK, cols] + far[:BLOCK] + extra
            retained[BLOCK:, here] = near_ref[BLOCK:, cols] + far[BLOCK:]
        done += carry_ref.shape[0]
    done = 0
    stores = []
    for j, start in enumerate(starts):
        silu_ref, count = refs[5 * j + 3], refs[5 * j + 4].shape[0]
        for g in range(count):
            here = columns(done + g)
            for t in range(blocks):
                rows = slice(t * BLOCK, (t + 1) * BLOCK)
                parted = retained[rows, here]
                variance = jnp.mean(parted * parted, axis=-1, keepdims=True)
                mixed_rows = silu_ref[rows, columns(g)] * (parted * lax.rsqrt(variance + EPSILON))
                rows_ref[rows, here] = mixed_rows.astype(BF16)
            target = out_ref.at[:, span(real_head(start, half) + g, 1)]
            stores.append(fetch(rows_ref.at[:, here], target, sems.at[done + g]))
        done += count
    for copy in stores:
        copy.wait()


def finish(starts, parts, carries, second, into=None):
    length = parts[0][0].shape[0]
    width = sum(carry.shape[0] for carry in carries) * BLOCK
    features = second.shape[0] * BLOCK
    operands = [x for part, carry in zip(parts, carries) for x in (*part, carry)] + [second]
    operands += [] if into is None else [into]
    return pl.pallas_call(
        functools.partial(finish_kernel, starts),
        in_specs=[HERE] * (len(operands) - (into is not None)) + ([] if into is None else [ANY]),
        out_specs=ANY,
        out_shape=jax.ShapeDtypeStruct((length, features), BF16),
        scratch_shapes=[
            pltpu.VMEM((length, width), F32),
            pltpu.VMEM((length, width), BF16),
            pltpu.SemaphoreType.DMA((width // BLOCK,)),
        ],
        input_output_aliases={} if into is None else {len(operands) - 1: 0},
        compiler_params=pltpu.CompilerParams(vmem_limit_bytes=10 * MIB),
        name=f"finish_{starts[0]}",
    )(*operands)


def mixed(a, x, b, y):
    total = a * x.astype(F32) + b * y.astype(F32)
    return total.astype(BF16)


def after(value, *others):
    return lax.optimization_barrier((value, *others))[0]


def per_device(queries, key_vectors, value_vectors, gate_input, norm_gain, decay_rate, band_reach):
    heads = decay_rate.shape[0]
    half = heads // 2
    few = half // 2
    chips = lax.axis_size("ctx")
    stay = functools.partial(pltpu.with_memory_space_constraint, memory_space=pltpu.HBM)
    keys, values = stay(key_vectors), stay(value_vectors)
    rates, reaches, gain = stay(decay_rate), stay(band_reach), norm_gain.reshape(-1, BLOCK)
    gates = gate_input

    own, away, seconds, keys, values, coefs, lines = block_states(keys, values, rates, reaches)
    to_mine, to_pair, chip_fade, is_first, is_last = [coefs[i] for i in range(5)]
    one = jnp.ones((1, 1, 1), F32)
    early, late = slice(0, few), slice(few, half)
    swap = lambda x: lax.ppermute(x, "rep", [(0, 1), (1, 0)])
    steps = [(i, i + 1) for i in range(2 * chips - 1)]
    onward = lambda x, pairs: lax.ppermute(x, ("ctx", "rep"), pairs)
    hop = lambda x, i: lax.ppermute(x, "ctx", [(i, i + 1)])
    step = lambda part, got: mixed(chip_fade[part], got, one, total[part])

    def shared(part, got):
        sent = mixed(to_mine[part], got, is_first[part], own[part])
        kept = mixed(to_pair[part], got, is_last[part], from_pair[part])
        return kept, swap(sent)

    from_pair = swap(away)
    across = [(3, 4)] if chips == 4 else steps
    second_first = onward(seconds, across)
    total = mixed(to_mine, own, to_pair, from_pair)
    b1 = hop(total[early], 0)
    a1 = hop(total[late], 0)
    if chips == 4:
        second_rest = onward(after(seconds, total), [pair for pair in steps if pair not in across])
        part0 = local_part(0, few, gain, after(queries, total), gates, lines, keys, values)
        b1, _ = lax.optimization_barrier((b1, part0[0]))
        t1 = step(early, b1)
        b2 = hop(t1, 1)
        local = lambda start, count, *others: local_part(
            start, count, gain, after(queries, *others), gates, lines, keys, values
        )
        part2 = local(half, few, t1)
        a1, _ = lax.optimization_barrier((a1, part2[0]))
        u1 = step(late, a1)
        a2 = hop(u1, 1)
        part1 = local(few, half - few, u1)
        b2, second_first, _ = lax.optimization_barrier((b2, second_first, part1[0]))
        t2 = step(early, b2)
        b3 = hop(t2, 2)
        part3 = local(half + few, half - few, t2)
        a2, _ = lax.optimization_barrier((a2, part3[0]))
        u2 = step(late, a2)
        a3 = hop(u2, 2)
        b3, second_rest, _ = lax.optimization_barrier((b3, second_rest, u2))
        second = second_first + second_rest
        got_b = b1 + b2 + b3
        kept_b, sent_b = shared(early, got_b)
        out = finish((0, half), (part0, part2), (kept_b, sent_b), second)
        a3, out = lax.optimization_barrier((a3, out))
        got_a = a1 + a2 + a3
    else:
        part0 = local_part(0, few, gain, queries, gates, lines, keys, values)
        local = lambda start, count: local_part(start, count, gain, queries, gates, lines, keys, values)
        got_a, got_b = arrived_a, arrived_b = a1, b1
        for i in range(1, chips - 1):
            arrived_a, arrived_b = hop(step(late, arrived_a), i), hop(step(early, arrived_b), i)
            got_a, got_b = got_a + arrived_a, got_b + arrived_b
        part1, part2, part3 = local(few, half - few), local(half, few), local(half + few, half - few)
        second = second_first
        kept_b, sent_b = shared(early, got_b)
        out = finish((0, half), (part0, part2), (kept_b, sent_b), second)
    kept_a, sent_a = shared(late, got_a)
    out = finish((few,), (part1,), (kept_a,), second, out)
    return finish((half + few,), (part3,), (sent_a,), second, out)


def solution(mesh):
    rows = P(("group", "ctx", "rep"), "head")
    return jax.shard_map(
        per_device,
        mesh=mesh,
        in_specs=(rows, rows, rows, rows, P("head"), P("head"), P("head")),
        out_specs=rows,
        check_vma=False,
    )
```

```python
import functools

import jax
import jax.numpy as jnp
from jax import lax
from jax.experimental import pallas as pl
from jax.experimental.pallas import tpu as pltpu
from jax.sharding import PartitionSpec as P

BLOCK = 128
REACH = 2
EPSILON = 1e-06
F32 = jnp.float32
BF16 = jnp.bfloat16
MIB = 1024 * 1024
CHUNK = 10
TRANS = (((0,), (0,)), ((), ()))
ROWS = (((1,), (1,)), ((), ()))
ANY = pl.BlockSpec(memory_space=pl.ANY)
HERE = pl.BlockSpec(memory_space=pltpu.VMEM)
SMEM = pltpu.SMEM


def chunk_of(heads):
    return max(g for g in range(1, CHUNK + 1) if heads % g == 0)


def row_offsets():
    return lax.broadcasted_iota(jnp.int32, (BLOCK, BLOCK), 0).astype(F32)


def power(rate, tokens):
    return jnp.exp(jnp.full((1, BLOCK), -tokens, F32) * rate)


def span(head, heads):
    return pl.ds(pl.multiple_of(head * BLOCK, BLOCK), heads * BLOCK)


def columns(g, heads=1):
    return slice(g * BLOCK, (g + heads) * BLOCK)


def centred(rows):
    return rows - jnp.mean(rows, axis=-1, keepdims=True)


def fetch(source, target, sem):
    copy = pltpu.make_async_copy(source, target, sem)
    copy.start()
    return copy


def real_head(relative, count):
    rep = lax.axis_index("rep")
    return rep * count + relative if relative < count else (1 - rep) * count + (relative - count)


def states_kernel(
    rate_in, reach_in, k_in, v_in, own_ref, away_ref, second_ref, k_ref, v_ref, coef_ref, row_ref,
    rates, reaches, sems,
):
    heads = k_ref.shape[1] // BLOCK
    count = heads // 2
    blocks = k_in.shape[0] // BLOCK
    chunk = chunk_of(count)
    small = [fetch(rate_in, rates, sems.at[0]), fetch(reach_in, reaches, sems.at[1])]
    loads = []
    for j in range(heads // chunk):
        where = span(real_head(j * chunk, count), chunk)
        here = columns(j * chunk, chunk)
        loads.append(fetch(k_in.at[:, where], k_ref.at[:, here], sems.at[2 + 2 * j]))
        loads.append(fetch(v_in.at[:, where], v_ref.at[:, here], sems.at[3 + 2 * j]))
    for copy in small:
        copy.wait()
    first = (lax.axis_index("rep") == 0).astype(F32)
    one = jnp.ones((1, BLOCK), F32)
    for g in range(heads):
        head = real_head(g, count)
        row_ref[0, g] = one * rates[head]
        row_ref[1, g] = one * reaches[head].astype(F32)
    for g in range(count):
        head = real_head(g, count)
        is_full = (reaches[head] > REACH).astype(F32)
        device = power(rates[head], blocks * BLOCK) * is_full
        chip = power(rates[head], 2 * blocks * BLOCK) * is_full
        rows = [first * device + (1.0 - first), first + (1.0 - first) * device, chip]
        for i, row in enumerate(rows + [one * first, one * (1.0 - first)]):
            coef_ref[i, g] = row
    offsets = row_offsets() - float(BLOCK)
    for g in range(heads):
        if g % chunk == 0:
            loads[2 * (g // chunk)].wait()
            loads[2 * (g // chunk) + 1].wait()
        head = real_head(g, count)
        rate = rates[head]
        reach = reaches[head]
        is_full = (reach > REACH).astype(F32)
        base = jnp.exp(offsets * rate)
        parts = []
        for t in range(blocks):
            faded = k_ref[t * BLOCK : (t + 1) * BLOCK, columns(g)].astype(F32) * base
            if t == blocks - 2:
                second = faded.astype(BF16)
            if t < blocks - 1:
                faded = faded * (power(rate, (blocks - 1 - t) * BLOCK) * is_full)
            parts.append(faded.astype(BF16))
        values = v_ref[:, columns(g)]
        carry = lax.dot_general(jnp.concatenate(parts, 0), values, TRANS, preferred_element_type=F32)
        carry = centred(carry).astype(BF16)
        if g < count:
            own_ref[g] = carry
        else:
            away_ref[g - count] = carry
        rows = values[(blocks - 2) * BLOCK : (blocks - 1) * BLOCK]
        state = lax.dot_general(second, rows, TRANS, preferred_element_type=F32)
        second_ref[g] = centred(state).astype(BF16)


def block_states(keys, values, rates, reaches):
    length, features = keys.shape
    heads = rates.shape[0]
    half = jax.ShapeDtypeStruct((heads // 2, BLOCK, BLOCK), BF16)
    rows = jax.ShapeDtypeStruct((length, features), BF16)
    coefs = jax.ShapeDtypeStruct((5, heads // 2, 1, BLOCK), F32)
    lines = jax.ShapeDtypeStruct((2, heads, 1, BLOCK), F32)
    return pl.pallas_call(
        states_kernel,
        in_specs=[ANY] * 4,
        out_specs=[HERE] * 7,
        out_shape=[half, half, jax.ShapeDtypeStruct((heads, BLOCK, BLOCK), BF16), rows, rows, coefs, lines],
        scratch_shapes=[
            SMEM(rates.shape, F32),
            SMEM(reaches.shape, jnp.int32),
            pltpu.SemaphoreType.DMA((2 + 2 * (heads // chunk_of(heads // 2)),)),
        ],
        compiler_params=pltpu.CompilerParams(vmem_limit_bytes=10 * MIB),
        name="block_states",
    )(rates, reaches, keys, values)


def local_kernel(
    start, gain_ref, q_ref, g_ref, row_ref, k_ref, v_ref, near_ref, faded_ref, second_ref, silu_ref, weights
):
    length = k_ref.shape[0]
    blocks = length // BLOCK
    count = near_ref.shape[1] // BLOCK
    first = real_head(start, k_ref.shape[1] // BLOCK // 2)
    offsets = row_offsets()
    gap = offsets - lax.broadcasted_iota(jnp.int32, (BLOCK, BLOCK), 1).astype(F32)
    causal = gap >= 0
    for g in range(count):
        rate = row_ref[0, start + g]
        reach = row_ref[1, start + g]
        fading = jnp.exp(gap * (-rate))
        tables = [jnp.where(causal, fading, 0.0)]
        for back in range(1, blocks):
            tables.append(fading * (power(rate, back * BLOCK) * (reach >= back).astype(F32)))
        fade = jnp.exp(offsets * (-rate))
        seconds = jnp.logical_and(reach >= 2, reach <= REACH).astype(F32)
        for t in range(blocks):
            rows = slice(t * BLOCK, (t + 1) * BLOCK)
            queries = q_ref[rows, span(first + g, 1)]
            scores = lax.dot_general(
                queries, k_ref[: (t + 1) * BLOCK, columns(start + g)], ROWS, preferred_element_type=F32
            )
            for u in range(t + 1):
                tile = slice(u * BLOCK, (u + 1) * BLOCK)
                weights[g, rows, tile] = (scores[:, tile] * tables[t - u]).astype(BF16)
            faded = queries.astype(F32) * fade
            faded_ref[rows, columns(g)] = (faded * (power(rate, t * BLOCK) * (reach > t).astype(F32))).astype(BF16)
            if t == 0:
                second_ref[:, columns(g)] = (faded * (power(rate, BLOCK) * seconds)).astype(BF16)
    for g in range(count):
        for t in range(blocks):
            rows = slice(t * BLOCK, (t + 1) * BLOCK)
            near = jnp.dot(
                weights[g, rows, : (t + 1) * BLOCK],
                v_ref[: (t + 1) * BLOCK, columns(start + g)],
                preferred_element_type=F32,
            )
            near_ref[rows, columns(g)] = centred(near)
    for g in range(count):
        gate = g_ref[:, span(first + g, 1)].astype(F32)
        silu_ref[:, columns(g)] = gate / (1.0 + jnp.exp(-gate)) * gain_ref[pl.ds(first + g, 1), :]


def local_part(start, count, gain, queries, gates, lines, keys, values):
    length = keys.shape[0]
    width = count * BLOCK
    rows = jax.ShapeDtypeStruct((length, width), BF16)
    wide = jax.ShapeDtypeStruct((length, width), F32)
    shapes = [wide, rows, jax.ShapeDtypeStruct((BLOCK, width), BF16), wide]
    return pl.pallas_call(
        functools.partial(local_kernel, start),
        in_specs=[HERE] * 6,
        out_specs=[HERE] * len(shapes),
        out_shape=shapes,
        scratch_shapes=[
            pltpu.VMEM((count, length, length), BF16),
        ],
        compiler_params=pltpu.CompilerParams(vmem_limit_bytes=14 * MIB),
        cost_estimate=pl.CostEstimate(flops=1, bytes_accessed=1, transcendentals=0),
        name=f"local_{start}",
    )(gain, queries, gates, lines, keys, values)


def finish_kernel(starts, *refs):
    second_ref = refs[5 * len(starts)]
    out_ref, retained, rows_ref, sems = refs[-4:]
    blocks = out_ref.shape[0] // BLOCK
    half = out_ref.shape[1] // BLOCK // 2
    done = 0
    for j, start in enumerate(starts):
        near_ref, faded_ref, factor_ref, _, carry_ref = refs[5 * j : 5 * j + 5]
        for g in range(carry_ref.shape[0]):
            cols = columns(g)
            here = columns(done + g)
            far = jnp.dot(faded_ref[:, cols], carry_ref[g], preferred_element_type=F32)
            extra = jnp.dot(factor_ref[:, cols], second_ref[(start + half) % (2 * half) + g], preferred_element_type=F32)
            retained[:BLOCK, here] = near_ref[:BLOCK, cols] + far[:BLOCK] + extra
            retained[BLOCK:, here] = near_ref[BLOCK:, cols] + far[BLOCK:]
        done += carry_ref.shape[0]
    done = 0
    stores = []
    for j, start in enumerate(starts):
        silu_ref, count = refs[5 * j + 3], refs[5 * j + 4].shape[0]
        for g in range(count):
            here = columns(done + g)
            for t in range(blocks):
                rows = slice(t * BLOCK, (t + 1) * BLOCK)
                parted = retained[rows, here]
                variance = jnp.mean(parted * parted, axis=-1, keepdims=True)
                mixed_rows = silu_ref[rows, columns(g)] * (parted * lax.rsqrt(variance + EPSILON))
                rows_ref[rows, here] = mixed_rows.astype(BF16)
            target = out_ref.at[:, span(real_head(start, half) + g, 1)]
            stores.append(fetch(rows_ref.at[:, here], target, sems.at[done + g]))
        done += count
    for copy in stores:
        copy.wait()


def finish(starts, parts, carries, second, into=None):
    length = parts[0][0].shape[0]
    width = sum(carry.shape[0] for carry in carries) * BLOCK
    features = second.shape[0] * BLOCK
    operands = [x for part, carry in zip(parts, carries) for x in (*part, carry)] + [second]
    operands += [] if into is None else [into]
    return pl.pallas_call(
        functools.partial(finish_kernel, starts),
        in_specs=[HERE] * (len(operands) - (into is not None)) + ([] if into is None else [ANY]),
        out_specs=ANY,
        out_shape=jax.ShapeDtypeStruct((length, features), BF16),
        scratch_shapes=[
            pltpu.VMEM((length, width), F32),
            pltpu.VMEM((length, width), BF16),
            pltpu.SemaphoreType.DMA((width // BLOCK,)),
        ],
        input_output_aliases={} if into is None else {len(operands) - 1: 0},
        compiler_params=pltpu.CompilerParams(vmem_limit_bytes=10 * MIB),
        name=f"finish_{starts[0]}",
    )(*operands)


def mixed(a, x, b, y):
    total = a * x.astype(F32) + b * y.astype(F32)
    return total.astype(BF16)


def after(value, *others):
    return lax.optimization_barrier((value, *others))[0]


def per_device(queries, key_vectors, value_vectors, gate_input, norm_gain, decay_rate, band_reach):
    heads = decay_rate.shape[0]
    half = heads // 2
    few = half // 2
    chips = lax.axis_size("ctx")
    stay = functools.partial(pltpu.with_memory_space_constraint, memory_space=pltpu.HBM)
    keys, values = stay(key_vectors), stay(value_vectors)
    rates, reaches, gain = stay(decay_rate), stay(band_reach), norm_gain.reshape(-1, BLOCK)
    gates = gate_input

    own, away, seconds, keys, values, coefs, lines = block_states(keys, values, rates, reaches)
    to_mine, to_pair, chip_fade, is_first, is_last = [coefs[i] for i in range(5)]
    one = jnp.ones((1, 1, 1), F32)
    early, late = slice(0, few), slice(few, half)
    swap = lambda x: lax.ppermute(x, "rep", [(0, 1), (1, 0)])
    steps = [(i, i + 1) for i in range(2 * chips - 1)]
    onward = lambda x, pairs: lax.ppermute(x, ("ctx", "rep"), pairs)
    hop = lambda x, i: lax.ppermute(x, "ctx", [(i, i + 1)])
    step = lambda part, got: mixed(chip_fade[part], got, one, total[part])

    def shared(part, got):
        sent = mixed(to_mine[part], got, is_first[part], own[part])
        kept = mixed(to_pair[part], got, is_last[part], from_pair[part])
        return kept, swap(sent)

    from_pair = swap(away)
    across = [(3, 4)] if chips == 4 else steps
    second_first = onward(seconds, across)
    total = mixed(to_mine, own, to_pair, from_pair)
    b1 = hop(total[early], 0)
    a1 = hop(total[late], 0)
    if chips == 4:
        second_rest = onward(after(seconds, total), [pair for pair in steps if pair not in across])
        part0 = local_part(0, few, gain, after(queries, total), gates, lines, keys, values)
        b1, _ = lax.optimization_barrier((b1, part0[0]))
        t1 = step(early, b1)
        b2 = hop(t1, 1)
        local = lambda start, count, *others: local_part(
            start, count, gain, after(queries, *others), gates, lines, keys, values
        )
        part2 = local(half, few, t1)
        a1, _ = lax.optimization_barrier((a1, part2[0]))
        u1 = step(late, a1)
        a2 = hop(u1, 1)
        part1 = local(few, half - few, u1)
        b2, second_first, _ = lax.optimization_barrier((b2, second_first, part1[0]))
        t2 = step(early, b2)
        b3 = hop(t2, 2)
        part3 = local(half + few, half - few, t2)
        a2, _ = lax.optimization_barrier((a2, part3[0]))
        u2 = step(late, a2)
        a3 = hop(u2, 2)
        b3, second_rest, _ = lax.optimization_barrier((b3, second_rest, u2))
        second = second_first + second_rest
        got_b = b1 + b2 + b3
        kept_b, sent_b = shared(early, got_b)
        out = finish((0, half), (part0, part2), (kept_b, sent_b), second)
        a3, out = lax.optimization_barrier((a3, out))
        got_a = a1 + a2 + a3
    else:
        part0 = local_part(0, few, gain, queries, gates, lines, keys, values)
        local = lambda start, count: local_part(start, count, gain, queries, gates, lines, keys, values)
        got_a, got_b = arrived_a, arrived_b = a1, b1
        for i in range(1, chips - 1):
            arrived_a, arrived_b = hop(step(late, arrived_a), i), hop(step(early, arrived_b), i)
            got_a, got_b = got_a + arrived_a, got_b + arrived_b
        part1, part2, part3 = local(few, half - few), local(half, few), local(half + few, half - few)
        second = second_first
        kept_b, sent_b = shared(early, got_b)
        out = finish((0, half), (part0, part2), (kept_b, sent_b), second)
    kept_a, sent_a = shared(late, got_a)
    out = finish((few,), (part1,), (kept_a,), second, out)
    return finish((half + few,), (part3,), (sent_a,), second, out)


def solution(mesh):
    rows = P(("group", "ctx", "rep"), "head")
    return jax.shard_map(
        per_device,
        mesh=mesh,
        in_specs=(rows, rows, rows, rows, P("head"), P("head"), P("head")),
        out_specs=rows,
        check_vma=False,
    )
```

```python
import functools

import jax
import jax.numpy as jnp
from jax import lax
from jax.experimental import pallas as pl
from jax.experimental.pallas import tpu as pltpu
from jax.sharding import PartitionSpec as P

BLOCK = 128
REACH = 2
EPSILON = 1e-06
F32 = jnp.float32
BF16 = jnp.bfloat16
MIB = 1024 * 1024
CHUNK = 10
TRANS = (((0,), (0,)), ((), ()))
ROWS = (((1,), (1,)), ((), ()))
ANY = pl.BlockSpec(memory_space=pl.ANY)
HERE = pl.BlockSpec(memory_space=pltpu.VMEM)
SMEM = pltpu.SMEM


def chunk_of(heads):
    return max(g for g in range(1, CHUNK + 1) if heads % g == 0)


def row_offsets():
    return lax.broadcasted_iota(jnp.int32, (BLOCK, BLOCK), 0).astype(F32)


def power(rate, tokens):
    return jnp.exp(jnp.full((1, BLOCK), -tokens, F32) * rate)


def span(head, heads):
    return pl.ds(pl.multiple_of(head * BLOCK, BLOCK), heads * BLOCK)


def columns(g, heads=1):
    return slice(g * BLOCK, (g + heads) * BLOCK)


def centred(rows):
    return rows - jnp.mean(rows, axis=-1, keepdims=True)


def fetch(source, target, sem):
    copy = pltpu.make_async_copy(source, target, sem)
    copy.start()
    return copy


def real_head(relative, count):
    rep = lax.axis_index("rep")
    return rep * count + relative if relative < count else (1 - rep) * count + (relative - count)


def states_kernel(
    rate_in, reach_in, k_in, v_in, own_ref, away_ref, second_ref, k_ref, v_ref, coef_ref, row_ref,
    rates, reaches, sems,
):
    heads = k_ref.shape[1] // BLOCK
    count = heads // 2
    blocks = k_in.shape[0] // BLOCK
    chunk = chunk_of(count)
    small = [fetch(rate_in, rates, sems.at[0]), fetch(reach_in, reaches, sems.at[1])]
    loads = []
    for j in range(heads // chunk):
        where = span(real_head(j * chunk, count), chunk)
        here = columns(j * chunk, chunk)
        loads.append(fetch(k_in.at[:, where], k_ref.at[:, here], sems.at[2 + 2 * j]))
        loads.append(fetch(v_in.at[:, where], v_ref.at[:, here], sems.at[3 + 2 * j]))
    for copy in small:
        copy.wait()
    first = (lax.axis_index("rep") == 0).astype(F32)
    one = jnp.ones((1, BLOCK), F32)
    for g in range(heads):
        head = real_head(g, count)
        row_ref[0, g] = one * rates[head]
        row_ref[1, g] = one * reaches[head].astype(F32)
    for g in range(count):
        head = real_head(g, count)
        is_full = (reaches[head] > REACH).astype(F32)
        device = power(rates[head], blocks * BLOCK) * is_full
        chip = power(rates[head], 2 * blocks * BLOCK) * is_full
        rows = [first * device + (1.0 - first), first + (1.0 - first) * device, chip]
        for i, row in enumerate(rows + [one * first, one * (1.0 - first)]):
            coef_ref[i, g] = row
    offsets = row_offsets() - float(BLOCK)
    for g in range(heads):
        if g % chunk == 0:
            loads[2 * (g // chunk)].wait()
            loads[2 * (g // chunk) + 1].wait()
        head = real_head(g, count)
        rate = rates[head]
        reach = reaches[head]
        is_full = (reach > REACH).astype(F32)
        base = jnp.exp(offsets * rate)
        parts = []
        for t in range(blocks):
            faded = k_ref[t * BLOCK : (t + 1) * BLOCK, columns(g)].astype(F32) * base
            if t == blocks - 2:
                second = faded.astype(BF16)
            if t < blocks - 1:
                faded = faded * (power(rate, (blocks - 1 - t) * BLOCK) * is_full)
            parts.append(faded.astype(BF16))
        values = v_ref[:, columns(g)]
        carry = lax.dot_general(jnp.concatenate(parts, 0), values, TRANS, preferred_element_type=F32)
        carry = centred(carry).astype(BF16)
        if g < count:
            own_ref[g] = carry
        else:
            away_ref[g - count] = carry
        rows = values[(blocks - 2) * BLOCK : (blocks - 1) * BLOCK]
        state = lax.dot_general(second, rows, TRANS, preferred_element_type=F32)
        second_ref[g] = centred(state).astype(BF16)


def block_states(keys, values, rates, reaches):
    length, features = keys.shape
    heads = rates.shape[0]
    half = jax.ShapeDtypeStruct((heads // 2, BLOCK, BLOCK), BF16)
    rows = jax.ShapeDtypeStruct((length, features), BF16)
    coefs = jax.ShapeDtypeStruct((5, heads // 2, 1, BLOCK), F32)
    lines = jax.ShapeDtypeStruct((2, heads, 1, BLOCK), F32)
    return pl.pallas_call(
        states_kernel,
        in_specs=[ANY] * 4,
        out_specs=[HERE] * 7,
        out_shape=[half, half, jax.ShapeDtypeStruct((heads, BLOCK, BLOCK), BF16), rows, rows, coefs, lines],
        scratch_shapes=[
            SMEM(rates.shape, F32),
            SMEM(reaches.shape, jnp.int32),
            pltpu.SemaphoreType.DMA((2 + 2 * (heads // chunk_of(heads // 2)),)),
        ],
        compiler_params=pltpu.CompilerParams(vmem_limit_bytes=10 * MIB),
        name="block_states",
    )(rates, reaches, keys, values)


def local_kernel(
    start, gain_ref, q_ref, g_ref, row_ref, k_ref, v_ref, near_ref, faded_ref, second_ref, silu_ref, weights
):
    length = k_ref.shape[0]
    blocks = length // BLOCK
    count = near_ref.shape[1] // BLOCK
    first = real_head(start, k_ref.shape[1] // BLOCK // 2)
    offsets = row_offsets()
    gap = offsets - lax.broadcasted_iota(jnp.int32, (BLOCK, BLOCK), 1).astype(F32)
    causal = gap >= 0
    for g in range(count):
        rate = row_ref[0, start + g]
        reach = row_ref[1, start + g]
        fading = jnp.exp(gap * (-rate))
        tables = [jnp.where(causal, fading, 0.0)]
        for back in range(1, blocks):
            tables.append(fading * (power(rate, back * BLOCK) * (reach >= back).astype(F32)))
        fade = jnp.exp(offsets * (-rate))
        seconds = jnp.logical_and(reach >= 2, reach <= REACH).astype(F32)
        for t in range(blocks):
            rows = slice(t * BLOCK, (t + 1) * BLOCK)
            queries = q_ref[rows, span(first + g, 1)]
            scores = lax.dot_general(
                queries, k_ref[: (t + 1) * BLOCK, columns(start + g)], ROWS, preferred_element_type=F32
            )
            for u in range(t + 1):
                tile = slice(u * BLOCK, (u + 1) * BLOCK)
                weights[g, rows, tile] = (scores[:, tile] * tables[t - u]).astype(BF16)
            faded = queries.astype(F32) * fade
            faded_ref[rows, columns(g)] = (faded * (power(rate, t * BLOCK) * (reach > t).astype(F32))).astype(BF16)
            if t == 0:
                second_ref[:, columns(g)] = (faded * (power(rate, BLOCK) * seconds)).astype(BF16)
    for g in range(count):
        for t in range(blocks):
            rows = slice(t * BLOCK, (t + 1) * BLOCK)
            near = jnp.dot(
                weights[g, rows, : (t + 1) * BLOCK],
                v_ref[: (t + 1) * BLOCK, columns(start + g)],
                preferred_element_type=F32,
            )
            near_ref[rows, columns(g)] = centred(near)
    for g in range(count):
        gate = g_ref[:, span(first + g, 1)].astype(F32)
        silu_ref[:, columns(g)] = gate / (1.0 + jnp.exp(-gate)) * gain_ref[pl.ds(first + g, 1), :]


def local_part(start, count, gain, queries, gates, lines, keys, values):
    length = keys.shape[0]
    width = count * BLOCK
    rows = jax.ShapeDtypeStruct((length, width), BF16)
    wide = jax.ShapeDtypeStruct((length, width), F32)
    shapes = [wide, rows, jax.ShapeDtypeStruct((BLOCK, width), BF16), wide]
    return pl.pallas_call(
        functools.partial(local_kernel, start),
        in_specs=[HERE] * 6,
        out_specs=[HERE] * len(shapes),
        out_shape=shapes,
        scratch_shapes=[
            pltpu.VMEM((count, length, length), BF16),
        ],
        compiler_params=pltpu.CompilerParams(vmem_limit_bytes=14 * MIB),
        cost_estimate=pl.CostEstimate(flops=1, bytes_accessed=1, transcendentals=0),
        name=f"local_{start}",
    )(gain, queries, gates, lines, keys, values)


def finish_kernel(starts, *refs):
    second_ref = refs[5 * len(starts)]
    out_ref, rows_ref, sems = refs[-3:]
    blocks = out_ref.shape[0] // BLOCK
    half = out_ref.shape[1] // BLOCK // 2
    done = 0
    stores = []
    for j, start in enumerate(starts):
        near_ref, faded_ref, factor_ref, silu_ref, carry_ref = refs[5 * j : 5 * j + 5]
        for g in range(carry_ref.shape[0]):
            cols = columns(g)
            here = columns(done)
            far = jnp.dot(faded_ref[:, cols], carry_ref[g], preferred_element_type=F32)
            sent_as = (start + half) % (2 * half) + g
            extra = jnp.dot(factor_ref[:, cols], second_ref[sent_as], preferred_element_type=F32)
            for t in range(blocks):
                rows = slice(t * BLOCK, (t + 1) * BLOCK)
                parted = near_ref[rows, cols] + far[rows]
                if t == 0:
                    parted = parted + extra
                variance = jnp.mean(parted * parted, axis=-1, keepdims=True)
                mixed_rows = silu_ref[rows, cols] * (parted * lax.rsqrt(variance + EPSILON))
                rows_ref[rows, here] = mixed_rows.astype(BF16)
            target = out_ref.at[:, span(real_head(start, half) + g, 1)]
            stores.append(fetch(rows_ref.at[:, here], target, sems.at[done]))
            done += 1
    for copy in stores:
        copy.wait()


def finish(starts, parts, carries, second, into=None):
    length = parts[0][0].shape[0]
    width = sum(carry.shape[0] for carry in carries) * BLOCK
    features = second.shape[0] * BLOCK
    operands = [x for part, carry in zip(parts, carries) for x in (*part, carry)] + [second]
    operands += [] if into is None else [into]
    return pl.pallas_call(
        functools.partial(finish_kernel, starts),
        in_specs=[HERE] * (len(operands) - (into is not None)) + ([] if into is None else [ANY]),
        out_specs=ANY,
        out_shape=jax.ShapeDtypeStruct((length, features), BF16),
        scratch_shapes=[
            pltpu.VMEM((length, width), BF16),
            pltpu.SemaphoreType.DMA((width // BLOCK,)),
        ],
        input_output_aliases={} if into is None else {len(operands) - 1: 0},
        compiler_params=pltpu.CompilerParams(vmem_limit_bytes=10 * MIB),
        name=f"finish_{starts[0]}",
    )(*operands)


def mixed(a, x, b, y):
    total = a * x.astype(F32) + b * y.astype(F32)
    return total.astype(BF16)


def after(value, *others):
    return lax.optimization_barrier((value, *others))[0]


def per_device(queries, key_vectors, value_vectors, gate_input, norm_gain, decay_rate, band_reach):
    heads = decay_rate.shape[0]
    half = heads // 2
    few = half // 2
    chips = lax.axis_size("ctx")
    stay = functools.partial(pltpu.with_memory_space_constraint, memory_space=pltpu.HBM)
    keys, values = stay(key_vectors), stay(value_vectors)
    rates, reaches, gain = stay(decay_rate), stay(band_reach), norm_gain.reshape(-1, BLOCK)
    gates = gate_input

    own, away, seconds, keys, values, coefs, lines = block_states(keys, values, rates, reaches)
    to_mine, to_pair, chip_fade, is_first, is_last = [coefs[i] for i in range(5)]
    one = jnp.ones((1, 1, 1), F32)
    early, late = slice(0, few), slice(few, half)
    swap = lambda x: lax.ppermute(x, "rep", [(0, 1), (1, 0)])
    steps = [(i, i + 1) for i in range(2 * chips - 1)]
    onward = lambda x, pairs: lax.ppermute(x, ("ctx", "rep"), pairs)
    hop = lambda x, i: lax.ppermute(x, "ctx", [(i, i + 1)])
    step = lambda part, got: mixed(chip_fade[part], got, one, total[part])

    def shared(part, got):
        sent = mixed(to_mine[part], got, is_first[part], own[part])
        kept = mixed(to_pair[part], got, is_last[part], from_pair[part])
        return kept, swap(sent)

    from_pair = swap(away)
    across = [(3, 4)] if chips == 4 else steps
    second_first = onward(seconds, across)
    total = mixed(to_mine, own, to_pair, from_pair)
    b1 = hop(total[early], 0)
    a1 = hop(total[late], 0)
    if chips == 4:
        second_rest = onward(after(seconds, total), [pair for pair in steps if pair not in across])
        part0 = local_part(0, few, gain, after(queries, total), gates, lines, keys, values)
        b1, _ = lax.optimization_barrier((b1, part0[0]))
        t1 = step(early, b1)
        b2 = hop(t1, 1)
        local = lambda start, count, *others: local_part(
            start, count, gain, after(queries, *others), gates, lines, keys, values
        )
        part2 = local(half, few, t1)
        a1, _ = lax.optimization_barrier((a1, part2[0]))
        u1 = step(late, a1)
        a2 = hop(u1, 1)
        part1 = local(few, half - few, u1)
        b2, second_first, _ = lax.optimization_barrier((b2, second_first, part1[0]))
        t2 = step(early, b2)
        b3 = hop(t2, 2)
        part3 = local(half + few, half - few, t2)
        a2, _ = lax.optimization_barrier((a2, part3[0]))
        u2 = step(late, a2)
        a3 = hop(u2, 2)
        b3, second_rest, _ = lax.optimization_barrier((b3, second_rest, u2))
        second = second_first + second_rest
        got_b = b1 + b2 + b3
        kept_b, sent_b = shared(early, got_b)
        out = finish((0, half), (part0, part2), (kept_b, sent_b), second)
        a3, out = lax.optimization_barrier((a3, out))
        got_a = a1 + a2 + a3
    else:
        part0 = local_part(0, few, gain, queries, gates, lines, keys, values)
        local = lambda start, count: local_part(start, count, gain, queries, gates, lines, keys, values)
        got_a, got_b = arrived_a, arrived_b = a1, b1
        for i in range(1, chips - 1):
            arrived_a, arrived_b = hop(step(late, arrived_a), i), hop(step(early, arrived_b), i)
            got_a, got_b = got_a + arrived_a, got_b + arrived_b
        part1, part2, part3 = local(few, half - few), local(half, few), local(half + few, half - few)
        second = second_first
        kept_b, sent_b = shared(early, got_b)
        out = finish((0, half), (part0, part2), (kept_b, sent_b), second)
    kept_a, sent_a = shared(late, got_a)
    out = finish((few,), (part1,), (kept_a,), second, out)
    return finish((half + few,), (part3,), (sent_a,), second, out)


def solution(mesh):
    rows = P(("group", "ctx", "rep"), "head")
    return jax.shard_map(
        per_device,
        mesh=mesh,
        in_specs=(rows, rows, rows, rows, P("head"), P("head"), P("head")),
        out_specs=rows,
        check_vma=False,
    )
```
